256 devices in a mesh: cfg: 2 (over core), fsdp: 8 (over x_hi, y), seq: 16 (over x_lo, z).
Axes of the slice: x: 4 (x_hi: 2, x_lo: 2; x = x_hi * 2 + x_lo), y: 4, z: 8, core: 2. Of those that a mesh axis runs over, the one named last changes fastest.
Arguments:
- query_act: bfloat16 [2, 8, 2048, 2048], P('cfg', 'fsdp', 'seq'), may hold values from -24 to 24
- key_act: bfloat16 [2, 8, 2048, 2048], P('cfg', 'fsdp', 'seq'), may hold values from -4 to 4
- value_act: bfloat16 [2, 8, 2048, 2048], P('cfg', 'fsdp', 'seq'), may hold values from -6 to 6
- out_weight: bfloat16 [2048, 1536], P(('fsdp', 'seq')), may hold values from -0.125 to 0.125
- reward_dir: bfloat16 [8, 2048, 1536], P('fsdp', 'seq'), may hold values from -6 to 6
- guide_index: int32 [1], replicated, may hold values from 0 to 127
- step_index: int32 [1], replicated, may hold values from 0 to 49
Outputs:
- guided: bfloat16 [8, 2048, 1536], P('fsdp', 'seq')
- grad_query: bfloat16 [2, 8, 2048, 2048], P('cfg', 'fsdp', 'seq')
- grad_key: bfloat16 [2, 8, 2048, 2048], P('cfg', 'fsdp', 'seq')
- grad_value: bfloat16 [2, 8, 2048, 2048], P('cfg', 'fsdp', 'seq')
- grad_weight: float32 [2048, 1536], P(('fsdp', 'seq'))
The draws below stay inside these ranges and needn't reach their ends.
All inputs are finite; a program needn't handle non-finite values.
Results may differ from the reference program's by a relative error of at most 0.01.
Values may be sent and summed in bfloat16 or wider, within the bound.
No kernel may reach another device: no remote copies, remote signals or barrier semaphores. Data moves between devices by JAX's collectives and lax.ppermute only.
A program may use at most 128 MiB of HBM per device.

```python
import jax
import jax.numpy as jnp
from jax import lax

HDIM = 128
DW = 1536
STEPS = 50
HD = 2048
SAMPLES = 8
TOKENS = 2048


def shared_keys(key):
    shape = (2, SAMPLES, TOKENS, HD)
    gauss = jnp.clip(jax.random.normal(key, shape, jnp.float32), -4.0, 4.0)
    keys_all = gauss
    for row in range(3):
        keys_all = keys_all.at[:, :, TOKENS - 4 - row, :].set(0.99 * keys_all[:, :, TOKENS - 1 - row, :])
    return keys_all


def draw_key_act(key, part):
    keys_all = shared_keys(key)
    return keys_all.astype(jnp.bfloat16)


def draw_query_act(key, part):
    shape = (2, SAMPLES, TOKENS, HD)
    key = jax.random.fold_in(key, 7)
    queries = 2.0 * jnp.clip(jax.random.normal(key, shape, jnp.float32), -4.0, 4.0)
    return queries.astype(jnp.bfloat16)


def shard_levels(rng, shape, shards, low, largest):
    def one(dim, blocks):
        steps = jax.random.uniform(jax.random.fold_in(jax.random.fold_in(rng, 6), dim), (blocks,), jnp.float32, low / len(shards), largest / len(shards))
        return jnp.repeat(jnp.exp(steps), shape[dim] // blocks).reshape((-1,) + (1,) * (len(shape) - dim - 1))

    factor_of = one(*shards[0])
    for cut in shards[1:]:
        factor_of = factor_of * one(*cut)
    return factor_of


def bell_draw(key, shape, scale, bound, split=(), kind=jnp.bfloat16):
    result = scale * jax.random.normal(key, shape, jnp.float32)
    if split:
        result = result * shard_levels(key, shape, split, -0.22, 0.18)
    return jnp.clip(result, -bound, bound).astype(kind)


def setup_inputs(seed: int = 0) -> dict:
    splits = jax.random.split(jax.random.key(seed), 8)
    return {
        "query_act": draw_query_act(jax.random.fold_in(splits[7], 71), 0),
        "key_act": draw_key_act(jax.random.fold_in(splits[7], 71), 0),
        "value_act": bell_draw(splits[2], (2, SAMPLES, TOKENS, HD), 1.0, 6.0, ((0, 2), (1, 8), (2, 16))),
        "out_weight": bell_draw(splits[3], (HD, DW), HD ** -0.5, 0.125, ((0, 128),)),
        "reward_dir": bell_draw(splits[4], (SAMPLES, TOKENS, DW), 1.0, 6.0, ((0, 8), (1, 16))),
        "guide_index": jax.random.randint(splits[5], (1,), 0, 128).astype(jnp.int32),
        "step_index": jax.random.randint(splits[6], (1,), 0, STEPS).astype(jnp.int32),
    }


GUIDE_STEP = 0.04


def reference(query_act, key_act, value_act, out_weight, reward_dir, guide_index, step_index):
    heads = HD // HDIM
    factor = HDIM ** -0.5

    def to_heads(array):
        array = array.reshape(2 * SAMPLES, TOKENS, heads, HDIM).transpose(0, 2, 1, 3)
        return array.reshape(2 * SAMPLES * heads, TOKENS, HDIM)

    def from_heads(array):
        array = array.reshape(2 * SAMPLES, heads, TOKENS, HDIM).transpose(0, 2, 1, 3)
        return array.reshape(2, SAMPLES, TOKENS, HD)

    queries, keys_all, values_all = to_heads(query_act), to_heads(key_act), to_heads(value_act)

    def forward_head(pack):
        qhead, khead, vhead = pack
        scores = jnp.dot(qhead, khead.T, preferred_element_type=jnp.float32) * factor
        peak = jnp.max(scores, axis=-1)
        weights = jnp.exp(scores - peak[:, None])
        total = jnp.sum(weights, axis=-1)
        probs = (weights / total[:, None]).astype(jnp.bfloat16)
        mixed = jnp.dot(probs, vhead, preferred_element_type=jnp.float32).astype(jnp.bfloat16)
        return mixed, peak, total

    mixed_h, peak, total = lax.map(forward_head, (queries, keys_all, values_all))
    mixed_all = from_heads(mixed_h)
    moment = step_index[0].astype(jnp.float32)
    gate = jnp.cos(0.5 * jnp.pi * (moment + 0.5) / STEPS)
    strength = 1.0 + GUIDE_STEP * guide_index[0].astype(jnp.float32)
    flat = mixed_all.reshape(-1, HD)
    proj = jnp.dot(flat, out_weight, preferred_element_type=jnp.float32)
    branch_out = lax.optimization_barrier((gate * proj).astype(jnp.bfloat16)).astype(jnp.float32)
    branch_out = branch_out.reshape(2, SAMPLES, TOKENS, DW)
    cond, uncond = branch_out[0], branch_out[1]
    guided = uncond + strength * (cond - uncond)
    resid = reward_dir.astype(jnp.float32) - guided
    coeff = jnp.stack([strength, 1.0 - strength]).reshape(2, 1, 1, 1)
    grad_out = ((gate * coeff) * resid[None]).astype(jnp.bfloat16).reshape(-1, DW)
    grad_mixed = lax.dot_general(grad_out, out_weight, (((1,), (1,)), ((), ())), preferred_element_type=jnp.float32)
    grad_mixed = grad_mixed.astype(jnp.bfloat16).reshape(2, SAMPLES, TOKENS, HD)
    grad_weight = lax.dot_general(flat, grad_out, (((0,), (0,)), ((), ())), preferred_element_type=jnp.float32)

    def backward_head(pack):
        qhead, khead, vhead, ohead, ghead, peak_h, total_h = pack
        scores = jnp.dot(qhead, khead.T, preferred_element_type=jnp.float32) * factor
        probs = jnp.exp(scores - peak_h[:, None]) / total_h[:, None]
        rounded = probs.astype(jnp.bfloat16)
        dvalue = jnp.dot(rounded.T, ghead, preferred_element_type=jnp.float32).astype(jnp.bfloat16)
        dprobs = jnp.dot(ghead, vhead.T, preferred_element_type=jnp.float32)
        inner = jnp.sum(ghead.astype(jnp.float32) * ohead.astype(jnp.float32), axis=-1)
        dscores = (probs * (dprobs - inner[:, None])).astype(jnp.bfloat16)
        dquery = (jnp.dot(dscores, khead, preferred_element_type=jnp.float32) * factor).astype(jnp.bfloat16)
        dkey = (jnp.dot(dscores.T, qhead, preferred_element_type=jnp.float32) * factor).astype(jnp.bfloat16)
        return dquery, dkey, dvalue

    dquery, dkey, dvalue = lax.map(backward_head, (queries, keys_all, values_all, mixed_h, to_heads(grad_mixed), peak, total))
    return guided.astype(jnp.bfloat16), from_heads(dquery), from_heads(dkey), from_heads(dvalue), grad_weight
```

```python
import functools

import jax
import jax.numpy as jnp
from jax import lax
from jax.experimental import pallas as pl
from jax.experimental.pallas import tpu as pltpu
from jax.sharding import PartitionSpec as P

HDIM = 128
STEPS = 50
GUIDE_STEP = 0.04
LOG2E = 1.4426950408889634
BF = jnp.bfloat16
F32 = jnp.float32
NT = (((1,), (1,)), ((), ()))
VMEM_LIMIT = 56 * 1024 * 1024


def params():
    return pltpu.CompilerParams(vmem_limit_bytes=VMEM_LIMIT)


def whole(count):
    return [pl.BlockSpec(memory_space=pltpu.VMEM) for _ in range(count)]


def pack_kernel(q_ref, k_ref, v_ref, out_ref):
    rows = q_ref.shape[0]
    for head in range(out_ref.shape[0]):
        lanes = slice(head * HDIM, (head + 1) * HDIM)
        for place, ref in enumerate((q_ref, k_ref, v_ref)):
            out_ref[head, place * rows : (place + 1) * rows, :] = ref[:, lanes]


def pack_heads(query, key, value):
    rows, width = query.shape
    return pl.pallas_call(
        pack_kernel,
        out_shape=jax.ShapeDtypeStruct((width // HDIM, 3 * rows, HDIM), BF),
        in_specs=whole(3),
        out_specs=whole(1)[0],
        compiler_params=params(),
        name="pack_heads",
    )(query, key, value)


def unpack_kernel(in_ref, q_ref, k_ref, v_ref):
    rows = q_ref.shape[0]
    for head in range(in_ref.shape[0]):
        lanes = slice(head * HDIM, (head + 1) * HDIM)
        for place, ref in enumerate((q_ref, k_ref, v_ref)):
            ref[:, lanes] = in_ref[head, place * rows : (place + 1) * rows, :]


def unpack_heads(packed):
    heads, rows3, _ = packed.shape
    shape = jax.ShapeDtypeStruct((rows3 // 3, heads * HDIM), BF)
    return pl.pallas_call(
        unpack_kernel,
        out_shape=(shape, shape, shape),
        in_specs=whole(1),
        out_specs=tuple(whole(3)),
        compiler_params=params(),
        name="unpack_heads",
    )(packed)


def forward_kernel(qkv_ref, out_ref, probs_ref, value_t):
    shards, rows3, _ = qkv_ref.shape
    rows = rows3 // 3
    length = shards * rows
    step = pl.program_id(0)
    take = out_ref.shape[0]

    @pl.when(step == 0)
    def _():
        value = qkv_ref[:, 2 * rows :, :].reshape(length, HDIM)
        value_t[...] = value.astype(F32).T.astype(BF)

    query = qkv_ref[pl.ds(step * take, take), :rows, :].reshape(take * rows, HDIM)
    keys = qkv_ref[:, rows : 2 * rows, :].reshape(length, HDIM)
    scores = lax.dot_general(keys, query, NT, preferred_element_type=F32)
    scale = HDIM ** (-0.5) * LOG2E
    peak = jnp.max(scores, axis=0, keepdims=True) * scale
    weights = jnp.exp2(scores * scale - peak)
    total = jnp.sum(weights, axis=0, keepdims=True)
    probs = (weights * (1.0 / total)).astype(BF)
    probs_ref[...] = probs
    mixed_t = jnp.dot(value_t[...], probs, preferred_element_type=F32)
    out_ref[...] = mixed_t.T.astype(BF).reshape(out_ref.shape)


def attend_forward(qkv):
    shards, rows3, _ = qkv.shape
    rows = rows3 // 3
    length = shards * rows
    take = 2
    return pl.pallas_call(
        forward_kernel,
        grid=(shards // take,),
        out_shape=(
            jax.ShapeDtypeStruct((shards, rows, HDIM), BF),
            jax.ShapeDtypeStruct((length, length), BF),
        ),
        in_specs=whole(1),
        out_specs=(
            pl.BlockSpec((take, rows, HDIM), lambda i: (i, 0, 0)),
            pl.BlockSpec((length, take * rows), lambda i: (0, i)),
        ),
        scratch_shapes=[pltpu.VMEM((HDIM, length), BF)],
        compiler_params=params(),
        name="attend_forward",
    )(qkv)


def backward_kernel(qkv_ref, mixed_ref, grad_ref, probs_ref, out_ref, inner, query_t):
    shards, rows3, _ = qkv_ref.shape
    rows = rows3 // 3
    length = shards * rows
    step = pl.program_id(0)
    block = probs_ref.shape[0]
    take = block // rows
    factor = HDIM ** (-0.5)
    grad = grad_ref[...].reshape(length, HDIM)

    @pl.when(step == 0)
    def _():
        mixed = mixed_ref[...].reshape(length, HDIM)
        product = grad.astype(F32) * mixed.astype(F32)
        inner[...] = jnp.sum(product.T, axis=0, keepdims=True)
        query_t[...] = jnp.zeros_like(query_t)

    query = qkv_ref[:, :rows, :].reshape(length, HDIM)
    here = pl.ds(step * take, take)
    keys = qkv_ref[here, rows : 2 * rows, :].reshape(block, HDIM)
    value = qkv_ref[here, 2 * rows :, :].reshape(block, HDIM)
    probs = probs_ref[...]
    grad_value = jnp.dot(probs, grad, preferred_element_type=F32)
    out_ref[here, 2 * rows :, :] = grad_value.astype(BF).reshape(take, rows, HDIM)
    grad_probs = lax.dot_general(value, grad, NT, preferred_element_type=F32)
    grad_scores = (probs.astype(F32) * (grad_probs - inner[...])).astype(BF)
    grad_key = jnp.dot(grad_scores, query, preferred_element_type=F32) * factor
    out_ref[here, rows : 2 * rows, :] = grad_key.astype(BF).reshape(take, rows, HDIM)
    keys_t = keys.astype(F32).T.astype(BF)
    query_t[...] += jnp.dot(keys_t, grad_scores, preferred_element_type=F32)

    @pl.when(step == pl.num_programs(0) - 1)
    def _():
        grad_query = (query_t[...] * factor).T.astype(BF)
        out_ref[:, :rows, :] = grad_query.reshape(shards, rows, HDIM)


def attend_backward(qkv, mixed, grad, probs):
    shards, rows3, _ = qkv.shape
    rows = rows3 // 3
    length = shards * rows
    take = 2
    return pl.pallas_call(
        backward_kernel,
        grid=(shards // take,),
        out_shape=jax.ShapeDtypeStruct(qkv.shape, BF),
        in_specs=whole(3) + [pl.BlockSpec((take * rows, length), lambda i: (i, 0))],
        out_specs=whole(1)[0],
        scratch_shapes=[pltpu.VMEM((1, length), F32), pltpu.VMEM((HDIM, length), F32)],
        compiler_params=params(),
        name="attend_backward",
    )(qkv, mixed, grad, probs)


def weight_blocks(refs):
    own, beside, left, right, far_own, far_beside = refs
    return [own[...], right[0], far_own[...], left[0], beside[...], right[1], far_beside[...], left[1]]


def columns_of(own_ref, other_ref, head):
    return jnp.concatenate(
        [
            jnp.concatenate([own_ref[head], own_ref[head + 1]], axis=1),
            jnp.concatenate([other_ref[head], other_ref[head + 1]], axis=1),
        ],
        axis=0,
    )


def project_kernel(
    place_ref, scalar_ref, own_ref, other_ref, reward_ref,
    w0, w1, w2, w3, w4, w5,
    guided_ref, grad_ref, keep_ref, send_ref,
):
    blocks = weight_blocks((w0, w1, w2, w3, w4, w5))
    rows = own_ref.shape[1]
    half = guided_ref.shape[1]
    first = place_ref[8] == 0
    gate, strength = scalar_ref[0], scalar_ref[1]
    total = None
    for place, block in enumerate(blocks):
        columns = columns_of(own_ref, other_ref, 2 * place_ref[place])
        part = jnp.dot(columns, block, preferred_element_type=F32)
        total = part if total is None else total + part
    branch_out = (gate * total).astype(BF).astype(F32)
    own_out, other_out = branch_out[:rows], branch_out[rows:]
    cond = jnp.where(first, own_out, other_out)
    uncond = jnp.where(first, other_out, own_out)
    guided = uncond + strength * (cond - uncond)
    guided_ref[...] = guided.astype(BF)
    reward = jnp.where(first, reward_ref[:, :half], reward_ref[:, half:]).astype(F32)
    resid = reward - guided
    own_coeff = gate * jnp.where(first, strength, 1.0 - strength)
    other_coeff = gate * jnp.where(first, 1.0 - strength, strength)
    grad = jnp.concatenate([own_coeff * resid, other_coeff * resid], axis=0).astype(BF)
    grad_ref[...] = grad
    for place, block in enumerate(blocks):
        head = 2 * place_ref[place]
        part = lax.dot_general(grad, block, NT, preferred_element_type=F32)
        for odd in range(2):
            lanes = part[:, odd * HDIM : (odd + 1) * HDIM]
            keep_ref[head + odd] = lanes[:rows]
            send_ref[head + odd] = lanes[rows:].astype(BF)


def project(place, scalars, own, other, reward, blocks):
    heads, rows, _ = own.shape
    half = reward.shape[1] // 2
    smem = pl.BlockSpec(memory_space=pltpu.SMEM)
    return pl.pallas_call(
        project_kernel,
        out_shape=(
            jax.ShapeDtypeStruct((rows, half), BF),
            jax.ShapeDtypeStruct((2 * rows, half), BF),
            jax.ShapeDtypeStruct((heads, rows, HDIM), F32),
            jax.ShapeDtypeStruct((heads, rows, HDIM), BF),
        ),
        in_specs=[smem, smem] + whole(3 + len(blocks)),
        out_specs=tuple(whole(4)),
        compiler_params=params(),
        name="project",
    )(place, scalars, own, other, reward, *blocks)


def weight_kernel(place_ref, own_ref, other_ref, grad_ref, here_ref, right_ref, far_ref, left_ref):
    grad = grad_ref[...]
    for place in range(8):
        columns = columns_of(own_ref, other_ref, 2 * place_ref[place])
        flipped = columns.astype(F32).T.astype(BF)
        part = jnp.dot(flipped, grad, preferred_element_type=F32)
        ref = (here_ref, right_ref, far_ref, left_ref)[place % 4]
        ref[place // 4] = part.astype(ref.dtype)


def weight_gradient(place, own, other, grad):
    shape = (2, 2 * HDIM, grad.shape[1])
    return pl.pallas_call(
        weight_kernel,
        out_shape=(
            jax.ShapeDtypeStruct(shape, F32),
            jax.ShapeDtypeStruct(shape, BF),
            jax.ShapeDtypeStruct(shape, BF),
            jax.ShapeDtypeStruct(shape, BF),
        ),
        in_specs=[pl.BlockSpec(memory_space=pltpu.SMEM)] + whole(3),
        out_specs=tuple(whole(4)),
        compiler_params=params(),
        name="weight_gradient",
    )(place, own, other, grad)


def shift_y(value, step):
    pairs = [(i, (i // 4) * 4 + (i % 4 + step) % 4) for i in range(8)]
    return lax.ppermute(value, "fsdp", pairs)


def swap(value, axis, mask):
    pairs = [(i, i ^ mask) for i in range(lax.axis_size(axis))]
    return lax.ppermute(value, axis, pairs)


SEQ_MASKS = (8, 4, 2, 1)


def gather_seq(part):
    place = lax.axis_index("seq")
    for mask in SEQ_MASKS[::-1]:
        got = swap(part, "seq", mask)
        low = (place & mask) == 0
        part = jnp.where(low, jnp.concatenate([part, got]), jnp.concatenate([got, part]))
    return part


def scatter_seq(part):
    place = lax.axis_index("seq")
    for mask in SEQ_MASKS:
        rows = part.shape[0] // 2
        low = (place & mask) == 0
        keep = jnp.where(low, part[:rows], part[rows:])
        send = jnp.where(low, part[rows:], part[:rows]).astype(BF)
        part = keep + swap(send, "seq", mask).astype(F32)
    return part


def gather_blocks(own):
    beside = swap(own, "fsdp", 4)
    pair = jnp.stack([own, beside])
    left = shift_y(pair, 1)
    right = shift_y(pair, -1)
    far_own = shift_y(left[0], 1)
    far_beside = shift_y(right[1], -1)
    return (own, beside, left, right, far_own, far_beside)


def scatter_blocks(here, right, far, left):
    from_left = shift_y(far[0], 1)
    from_right = shift_y(far[1], -1)
    to_right = jnp.stack([(right[0].astype(F32) + from_left.astype(F32)).astype(BF), right[1]])
    to_left = jnp.stack([left[0], (left[1].astype(F32) + from_right.astype(F32)).astype(BF)])
    got_left = shift_y(to_right, 1)
    got_right = shift_y(to_left, -1)
    here = here + got_left.astype(F32) + got_right.astype(F32)
    return here[0] + swap(here[1].astype(BF), "fsdp", 4).astype(F32)


def over_seq(array):
    return lax.all_to_all(array, "seq", split_axis=0, concat_axis=0, tiled=True)


def joined(own, other, first):
    return jnp.where(
        first,
        jnp.concatenate([own, other], axis=1),
        jnp.concatenate([other, own], axis=1),
    )


def local(query_act, key_act, value_act, out_weight, reward_dir, guide_index, step_index):
    cfg = lax.axis_index("cfg")
    first = cfg == 0
    fsdp = lax.axis_index("fsdp")
    place = jnp.stack(
        [((fsdp // 4) ^ (r // 4)) * 4 + (fsdp + r) % 4 for r in range(8)] + [cfg]
    ).astype(jnp.int32)
    moment = step_index[0].astype(F32)
    gate = jnp.cos(0.5 * jnp.pi * (moment + 0.5) / STEPS)
    strength = 1.0 + GUIDE_STEP * guide_index[0].astype(F32)
    scalars = jnp.stack([gate, strength])

    half = out_weight.shape[1] // 2
    qkv = over_seq(pack_heads(query_act[0, 0], key_act[0, 0], value_act[0, 0]))
    own_half = jnp.where(first, out_weight[:, :half], out_weight[:, half:])
    blocks = gather_blocks(gather_seq(own_half))
    mixed_h, probs = attend_forward(qkv)
    mixed = over_seq(mixed_h)
    mixed_other = swap(mixed, "cfg", 1)
    guided, grad_out, keep, send = project(
        place, scalars, mixed, mixed_other, reward_dir[0], blocks
    )
    grad_mixed = (keep + swap(send, "cfg", 1).astype(F32)).astype(BF)
    grad_h = over_seq(grad_mixed)
    parts = weight_gradient(place, mixed, mixed_other, grad_out)
    grad_half = scatter_seq(scatter_blocks(*parts))
    grad_weight = joined(grad_half, swap(grad_half, "cfg", 1), first)
    guided_all = joined(guided, swap(guided, "cfg", 1), first)
    packed = over_seq(attend_backward(qkv, mixed_h, grad_h, probs))
    grad_query, grad_key, grad_value = unpack_heads(packed)
    return (
        guided_all[None],
        grad_query[None, None],
        grad_key[None, None],
        grad_value[None, None],
        grad_weight,
    )


def solution(mesh):
    placed = (
        P("cfg", "fsdp", "seq", None),
        P("cfg", "fsdp", "seq", None),
        P("cfg", "fsdp", "seq", None),
        P(("fsdp", "seq"), None),
        P("fsdp", "seq", None),
        P(),
        P(),
    )
    return jax.shard_map(
        local,
        mesh=mesh,
        in_specs=placed,
        out_specs=(
            P("fsdp", "seq", None),
            P("cfg", "fsdp", "seq", None),
            P("cfg", "fsdp", "seq", None),
            P("cfg", "fsdp", "seq", None),
            P(("fsdp", "seq"), None),
        ),
        check_vma=False,
    )
```

```python
import functools

import jax
import jax.numpy as jnp
from jax import lax
from jax.experimental import pallas as pl
from jax.experimental.pallas import tpu as pltpu
from jax.sharding import PartitionSpec as P

HDIM = 128
STEPS = 50
GUIDE_STEP = 0.04
LOG2E = 1.4426950408889634
BF = jnp.bfloat16
F32 = jnp.float32
NT = (((1,), (1,)), ((), ()))
VMEM_LIMIT = 56 * 1024 * 1024
EXTRA = 48


def params():
    return pltpu.CompilerParams(vmem_limit_bytes=VMEM_LIMIT)


def whole(count):
    return [pl.BlockSpec(memory_space=pltpu.VMEM) for _ in range(count)]


def anywhere():
    return pl.BlockSpec(memory_space=pl.ANY)


def scalars_spec():
    return pl.BlockSpec(memory_space=pltpu.SMEM)


def call(kernel, name, out_shape, in_specs, out_specs=None, **kwargs):
    if out_specs is None:
        out_specs = whole(len(out_shape)) if isinstance(out_shape, tuple) else whole(1)[0]
    return pl.pallas_call(
        kernel,
        out_shape=out_shape,
        in_specs=in_specs,
        out_specs=tuple(out_specs) if isinstance(out_shape, tuple) else out_specs,
        compiler_params=params(),
        name=name,
        **kwargs,
    )


def shaped(shape, dtype=BF):
    return jax.ShapeDtypeStruct(shape, dtype)


def lanes_of(head):
    return slice(head * HDIM, (head + 1) * HDIM)


def pack_first_kernel(place_ref, q_ref, k_ref, w_ref, out_ref):
    rows = q_ref.shape[0]
    deep = w_ref.shape[0]
    first = place_ref[0] == 0
    half = w_ref.shape[1] // 2
    picked = jnp.where(first, w_ref[:, :half], w_ref[:, half:])
    heads = out_ref.shape[0]
    per = EXTRA // deep
    for head in range(heads):
        side = head // (heads // 2)
        for part in range(per):
            out_ref[head, part * deep : (part + 1) * deep, :] = picked[:, lanes_of(side * per + part)]
        out_ref[head, EXTRA : EXTRA + rows, :] = q_ref[:, lanes_of(head)]
        out_ref[head, EXTRA + rows :, :] = k_ref[:, lanes_of(head)]


def pack_first(place, query, key, weight):
    rows, width = query.shape
    return call(
        pack_first_kernel,
        "pack_first",
        shaped((width // HDIM, EXTRA + 2 * rows, HDIM)),
        [scalars_spec()] + whole(3),
    )(place, query, key, weight)


def pack_kernel(in_ref, out_ref):
    for head in range(out_ref.shape[0]):
        out_ref[head] = in_ref[:, lanes_of(head)]


def pack_heads(array):
    rows, width = array.shape
    return call(pack_kernel, "pack_heads", shaped((width // HDIM, rows, HDIM)), whole(1))(array)


def unpack_kernel(in_ref, *out_refs):
    rows = out_refs[0].shape[0]
    skip = in_ref.shape[1] - rows * len(out_refs)
    for head in range(in_ref.shape[0]):
        for place, ref in enumerate(out_refs):
            start = skip + place * rows
            ref[:, lanes_of(head)] = in_ref[head, start : start + rows, :]


def unpack_heads(packed, count, rows):
    out = shaped((rows, packed.shape[0] * HDIM))
    return call(unpack_kernel, "unpack_heads", (out,) * count, whole(1))(packed)


def extra_spec(packed):
    return pl.BlockSpec((packed.shape[0], EXTRA, HDIM), lambda i: (0, 0, 0))


def piece_kernel(in_ref, out_ref):
    per = out_ref.shape[1] // HDIM
    deep = EXTRA // per
    for source in range(in_ref.shape[0]):
        for part in range(per):
            out_ref[source * deep : (source + 1) * deep, lanes_of(part)] = in_ref[
                source, part * deep : (part + 1) * deep, :
            ]


def weight_piece(packed, deep):
    return call(
        piece_kernel,
        "weight_piece",
        shaped((packed.shape[0] * deep, EXTRA // deep * HDIM)),
        [extra_spec(packed)],
        grid=(1,),
    )(packed)


def probs_kernel(first_ref, order_ref, probs_ref):
    shards, total_rows, _ = first_ref.shape
    rows = (total_rows - EXTRA) // 2
    length = shards * rows
    step = pl.program_id(0)
    take = probs_ref.shape[1] // rows
    query = first_ref[pl.ds(step * take, take), EXTRA : EXTRA + rows, :].reshape(take * rows, HDIM)
    keys = first_ref[:, EXTRA + rows :, :].reshape(length, HDIM)
    scores = lax.dot_general(keys, query, NT, preferred_element_type=F32)
    scale = HDIM ** (-0.5) * LOG2E
    peak = jnp.max(scores, axis=0, keepdims=True) * scale
    weights = jnp.exp2(scores * scale - peak)
    total = jnp.sum(weights, axis=0, keepdims=True)
    probs_ref[...] = (weights * (1.0 / total)).astype(BF)


def probabilities(first, order):
    shards, total_rows, _ = first.shape
    rows = (total_rows - EXTRA) // 2
    length = shards * rows
    take = 2
    return call(
        probs_kernel,
        "probabilities",
        shaped((length, length)),
        whole(1) + [anywhere()],
        pl.BlockSpec((length, take * rows), lambda i: (0, i)),
        grid=(shards // take,),
    )(first, order)


def mix_kernel(value_ref, probs_ref, out_ref, value_t):
    shards, rows, _ = value_ref.shape

    @pl.when(pl.program_id(0) == 0)
    def _():
        value_t[...] = value_ref[...].reshape(shards * rows, HDIM).astype(F32).T.astype(BF)

    mixed_t = jnp.dot(value_t[...], probs_ref[...], preferred_element_type=F32)
    out_ref[...] = mixed_t.T.astype(BF).reshape(out_ref.shape)


def mix(value, probs):
    shards, rows, _ = value.shape
    length = shards * rows
    take = 2
    return call(
        mix_kernel,
        "mix",
        shaped(value.shape),
        whole(1) + [pl.BlockSpec((length, take * rows), lambda i: (0, i))],
        pl.BlockSpec((take, rows, HDIM), lambda i: (i, 0, 0)),
        grid=(shards // take,),
        scratch_shapes=[pltpu.VMEM((HDIM, length), BF)],
    )(value, probs)


def grad_value_kernel(grad_ref, probs_ref, out_ref):
    shards, rows, _ = grad_ref.shape
    grad = grad_ref[...].reshape(shards * rows, HDIM)
    part = jnp.dot(probs_ref[...], grad, preferred_element_type=F32)
    out_ref[...] = part.astype(BF).reshape(out_ref.shape)


def grad_of_value(grad, probs):
    shards, rows, _ = grad.shape
    length = shards * rows
    take = 2
    return call(
        grad_value_kernel,
        "grad_of_value",
        shaped(grad.shape),
        whole(1) + [pl.BlockSpec((take * rows, length), lambda i: (i, 0))],
        pl.BlockSpec((take, rows, HDIM), lambda i: (i, 0, 0)),
        grid=(shards // take,),
    )(grad, probs)


def backward_kernel(first_ref, value_ref, mixed_ref, grad_ref, order_ref, probs_ref, out_ref, inner, query_t):
    shards, rows, _ = value_ref.shape
    length = shards * rows
    step = pl.program_id(0)
    block = probs_ref.shape[0]
    take = block // rows
    factor = HDIM ** (-0.5)
    grad = grad_ref[...].reshape(length, HDIM)

    @pl.when(step == 0)
    def _():
        mixed = mixed_ref[...].reshape(length, HDIM)
        product = grad.astype(F32) * mixed.astype(F32)
        inner[...] = jnp.sum(product.T, axis=0, keepdims=True)
        query_t[...] = jnp.zeros_like(query_t)

    query = first_ref[:, EXTRA : EXTRA + rows, :].reshape(length, HDIM)
    here = pl.ds(step * take, take)
    keys = first_ref[here, EXTRA + rows :, :].reshape(block, HDIM)
    value = value_ref[here].reshape(block, HDIM)
    probs = probs_ref[...]
    grad_probs = lax.dot_general(value, grad, NT, preferred_element_type=F32)
    grad_scores = (probs.astype(F32) * (grad_probs - inner[...])).astype(BF)
    grad_key = jnp.dot(grad_scores, query, preferred_element_type=F32) * factor
    out_ref[here, EXTRA + rows :, :] = grad_key.astype(BF).reshape(take, rows, HDIM)
    keys_t = keys.astype(F32).T.astype(BF)
    query_t[...] += jnp.dot(keys_t, grad_scores, preferred_element_type=F32)

    @pl.when(step == pl.num_programs(0) - 1)
    def _():
        grad_query = (query_t[...] * factor).T.astype(BF)
        out_ref[:, EXTRA : EXTRA + rows, :] = grad_query.reshape(shards, rows, HDIM)
        out_ref[:, :EXTRA, :] = jnp.zeros((shards, EXTRA, HDIM), BF)


def attend_backward(first, value, mixed, grad, order, probs):
    shards, rows, _ = value.shape
    length = shards * rows
    take = 2
    return call(
        backward_kernel,
        "attend_backward",
        shaped(first.shape),
        whole(4) + [anywhere(), pl.BlockSpec((take * rows, length), lambda i: (i, 0))],
        whole(1)[0],
        grid=(shards // take,),
        scratch_shapes=[pltpu.VMEM((1, length), F32), pltpu.VMEM((HDIM, length), F32)],
    )(first, value, mixed, grad, order, probs)


def piece_place(place_ref, slot):
    block = place_ref[1 + 2 * slot]
    side = place_ref[2 + 2 * slot]
    return block, side


def assemble_kernel(place_ref, *refs):
    pairs, out_ref, sems = refs[:8], refs[8], refs[9]
    deep, wide = pairs[0].shape[1:]
    copies = []
    for slot in range(16):
        block, side = piece_place(place_ref, slot)
        rows = pl.ds(pl.multiple_of(block * deep, deep), deep)
        lanes = pl.ds(pl.multiple_of(side * wide, HDIM), wide)
        copies.append(
            pltpu.make_async_copy(
                pairs[slot // 2].at[slot % 2], out_ref.at[rows, lanes], sems.at[slot]
            )
        )
    for copy in copies:
        copy.start()
    for copy in copies:
        copy.wait()


def assemble(place, pairs):
    _, deep, wide = pairs[0].shape
    return call(
        assemble_kernel,
        "assemble",
        shaped((8 * deep, 2 * wide)),
        [scalars_spec()] + [anywhere()] * 8,
        anywhere(),
        scratch_shapes=[pltpu.SemaphoreType.DMA((16,))],
    )(place, *pairs)


def side_by_side(ref):
    return jnp.concatenate([ref[head] for head in range(ref.shape[0])], axis=1)


def project_kernel(
    place_ref, scalar_ref, own_ref, other_ref, reward_ref, weight_ref,
    guided_ref, grad_ref, keep_ref, send_ref, held, sems,
):
    rows = own_ref.shape[1]
    half = guided_ref.shape[1]
    heads = own_ref.shape[0]
    blocks = heads // 2
    deep = 2 * HDIM
    copies = []
    for block in range(blocks):
        span = pl.ds(block * deep, deep)
        copies.append(pltpu.make_async_copy(weight_ref.at[span], held.at[span], sems.at[block]))
    for copy in copies:
        copy.start()
    first = place_ref[0] == 0
    gate, strength = scalar_ref[0], scalar_ref[1]
    total = None
    for block in range(blocks):
        head = 2 * block
        columns = jnp.concatenate(
            [
                jnp.concatenate([own_ref[head], own_ref[head + 1]], axis=1),
                jnp.concatenate([other_ref[head], other_ref[head + 1]], axis=1),
            ],
            axis=0,
        )
        copies[block].wait()
        part = jnp.dot(
            columns, held[block * deep : (block + 1) * deep], preferred_element_type=F32
        )
        total = part if total is None else total + part
    branch_out = (gate * total).astype(BF).astype(F32)
    own_out, other_out = branch_out[:rows], branch_out[rows:]
    cond = jnp.where(first, own_out, other_out)
    uncond = jnp.where(first, other_out, own_out)
    guided = uncond + strength * (cond - uncond)
    guided_ref[...] = guided.astype(BF)
    reward = jnp.where(first, reward_ref[:, :half], reward_ref[:, half:]).astype(F32)
    resid = reward - guided
    own_coeff = gate * jnp.where(first, strength, 1.0 - strength)
    other_coeff = gate * jnp.where(first, 1.0 - strength, strength)
    grad = jnp.concatenate([own_coeff * resid, other_coeff * resid], axis=0).astype(BF)
    grad_ref[...] = grad
    for block in range(blocks):
        part = lax.dot_general(
            grad, held[block * deep : (block + 1) * deep], NT, preferred_element_type=F32
        )
        for odd in range(2):
            lanes = part[:, lanes_of(odd)]
            keep_ref[2 * block + odd] = lanes[:rows]
            send_ref[2 * block + odd] = lanes[rows:].astype(BF)


def project(place, scalars, own, other, reward, weight):
    heads, rows, _ = own.shape
    half = reward.shape[1] // 2
    return call(
        project_kernel,
        "project",
        (
            shaped((rows, half)),
            shaped((2 * rows, half)),
            shaped((heads, rows, HDIM), F32),
            shaped((heads, rows, HDIM)),
        ),
        [scalars_spec(), scalars_spec()] + whole(3) + [anywhere()],
        scratch_shapes=[
            pltpu.VMEM(weight.shape, BF),
            pltpu.SemaphoreType.DMA((heads // 2,)),
        ],
    )(place, scalars, own, other, reward, weight)


def weight_kernel(place_ref, own_ref, other_ref, grad_ref, *refs):
    pairs, held, sems = refs[:8], refs[8], refs[9]
    deep, wide = pairs[0].shape[1:]
    grad = grad_ref[...]
    for head in range(own_ref.shape[0]):
        flipped = jnp.concatenate(
            [own_ref[head].astype(F32).T.astype(BF), other_ref[head].astype(F32).T.astype(BF)], axis=1
        )
        part = jnp.dot(flipped, grad, preferred_element_type=F32)
        held[head * HDIM : (head + 1) * HDIM] = part.astype(BF)
    copies = []
    for slot in range(16):
        block, side = piece_place(place_ref, slot)
        rows = pl.ds(pl.multiple_of(block * deep, deep), deep)
        lanes = pl.ds(pl.multiple_of(side * wide, HDIM), wide)
        copies.append(
            pltpu.make_async_copy(
                held.at[rows, lanes], pairs[slot // 2].at[slot % 2], sems.at[slot]
            )
        )
    for copy in copies:
        copy.start()
    for copy in copies:
        copy.wait()


def weight_gradient(place, own, other, grad):
    heads = own.shape[0]
    half = grad.shape[1]
    pair = shaped((2, 2 * HDIM, half // 2))
    return call(
        weight_kernel,
        "weight_gradient",
        (pair,) * 8,
        [scalars_spec()] + whole(3),
        [anywhere()] * 8,
        scratch_shapes=[
            pltpu.VMEM((heads * HDIM, half), BF),
            pltpu.SemaphoreType.DMA((16,)),
        ],
    )(place, own, other, grad)


def add_kernel(keep_ref, got_ref, order_ref, out_ref):
    out_ref[...] = (keep_ref[...] + got_ref[...].astype(F32)).astype(BF)


def add_after(keep, got, order):
    return call(add_kernel, "add_after", shaped(got.shape), whole(2) + [anywhere()])(keep, got, order)


def fill_kernel(here_ref, left_ref, right_ref, packed_ref, order_ref, out_ref, held, sem):
    per = here_ref.shape[1] // HDIM
    deep = EXTRA // per
    total = here_ref[...] + left_ref[...].astype(F32) + right_ref[...].astype(F32)
    total = total.astype(BF)
    for target in range(held.shape[0]):
        for part in range(per):
            held[target, part * deep : (part + 1) * deep, :] = total[
                target * deep : (target + 1) * deep, lanes_of(part)
            ]
    copy = pltpu.make_async_copy(held, out_ref.at[:, pl.ds(0, EXTRA), :], sem)
    copy.start()
    copy.wait()


def fill_extra(here, left, right, packed, order):
    return call(
        fill_kernel,
        "fill_extra",
        shaped(packed.shape),
        whole(3) + [anywhere()] * 2,
        anywhere(),
        input_output_aliases={3: 0},
        scratch_shapes=[
            pltpu.VMEM((packed.shape[0], EXTRA, HDIM), BF),
            pltpu.SemaphoreType.DMA,
        ],
    )(here, left, right, packed, order)


def sum_kernel(in_ref, out_ref):
    sources = in_ref.shape[0]
    deep = out_ref.shape[0]
    per = EXTRA // deep
    for side in range(2):
        for part in range(per):
            rows = slice(part * deep, (part + 1) * deep)
            total = None
            for source in range(sources // 2):
                piece = in_ref[side * (sources // 2) + source, rows, :].astype(F32)
                total = piece if total is None else total + piece
            out_ref[:, lanes_of(side * per + part)] = total


def sum_extra(packed, deep):
    return call(
        sum_kernel,
        "sum_extra",
        shaped((deep, 2 * (EXTRA // deep) * HDIM), F32),
        [extra_spec(packed)],
        grid=(1,),
    )(packed)


def swap_cfg(value):
    return lax.ppermute(value, "cfg", [(0, 1), (1, 0)])


def shift_y(value, step):
    pairs = [(i, (i // 4) * 4 + (i % 4 + step) % 4) for i in range(8)]
    return lax.ppermute(value, "fsdp", pairs)


def shift_x(value, step):
    pairs = []
    for fsdp in range(8):
        for seq in range(16):
            x = ((fsdp // 4) * 2 + seq // 8 + step) % 4
            target = ((x // 2) * 4 + fsdp % 4) * 16 + (x % 2) * 8 + seq % 8
            pairs.append((fsdp * 16 + seq, target))
    return lax.ppermute(value, ("fsdp", "seq"), pairs)


def gather_pairs(piece):
    half = piece.shape[0] // 2
    left = shift_x(piece, 1)
    right = shift_x(piece, -1)
    far_top = shift_x(left[:half], 1)
    far_low = shift_x(right[half:], -1)
    near = jnp.stack([piece, right])
    past = jnp.stack([jnp.concatenate([far_top, far_low]), left])
    near_left, near_right = shift_y(near, 1), shift_y(near, -1)
    past_left, past_right = shift_y(past, 1), shift_y(past, -1)
    near_far = shift_y(near_left, 1)
    past_far = shift_y(past_right, -1)
    return (near, past, near_right, past_right, near_far, past_far, near_left, past_left)


def added(one, two):
    return (one.astype(F32) + two.astype(F32)).astype(BF)


def scatter_pairs(pairs):
    near, past, near_right, past_right, near_far, past_far, near_left, past_left = pairs
    from_left = shift_y(near_far, 1)
    from_right = shift_y(past_far, -1)
    got_past = shift_y(past_right, 1)
    got_near = shift_y(near_left, -1)
    got_near_too = shift_y(added(near_right, from_left), 1)
    got_past_too = shift_y(added(past_left, from_right), -1)
    near = near.astype(F32) + got_near.astype(F32) + got_near_too.astype(F32)
    past = past.astype(F32) + got_past.astype(F32) + got_past_too.astype(F32)
    here, right, far, left = near[0], near[1], past[0].astype(BF), past[1]
    half = far.shape[0] // 2
    got_top = shift_x(far[:half], 1).astype(F32)
    got_low = shift_x(far[half:], -1).astype(F32)
    right = jnp.concatenate([right[:half] + got_top, right[half:]]).astype(BF)
    left = jnp.concatenate([left[:half], left[half:] + got_low]).astype(BF)
    return here, shift_x(right, 1), shift_x(left, -1)


def over_seq(array):
    return lax.all_to_all(array, "seq", split_axis=0, concat_axis=0, tiled=True)


def joined(own, other, first):
    return jnp.where(
        first,
        jnp.concatenate([own, other], axis=1),
        jnp.concatenate([other, own], axis=1),
    )


def places():
    cfg = lax.axis_index("cfg")
    fsdp = lax.axis_index("fsdp")
    x = (fsdp >> 2) * 2 + (lax.axis_index("seq") >> 3)
    y = fsdp & 3
    slots = jnp.arange(16)
    there = (x + (slots & 3)) & 3
    block = (there >> 1) * 4 + ((y + (slots >> 2)) & 3)
    table = jnp.stack([block, there & 1], axis=1).reshape(-1)
    return jnp.concatenate([cfg[None], table]).astype(jnp.int32)


def local(query_act, key_act, value_act, out_weight, reward_dir, guide_index, step_index):
    place = places()
    first_core = place[0] == 0
    moment = step_index[0].astype(F32)
    gate = jnp.cos(0.5 * jnp.pi * (moment + 0.5) / STEPS)
    strength = 1.0 + GUIDE_STEP * guide_index[0].astype(F32)
    scalars = jnp.stack([gate, strength])
    deep = out_weight.shape[0]
    rows = query_act.shape[2]

    first = over_seq(pack_first(place, query_act[0, 0], key_act[0, 0], out_weight))
    value = over_seq(pack_heads(value_act[0, 0]))
    piece = weight_piece(first, deep)
    weight = assemble(place, gather_pairs(piece))
    probs = probabilities(first, piece)
    mixed_h = mix(value, probs)
    mixed = over_seq(mixed_h)
    mixed_other = swap_cfg(mixed)
    guided, grad_out, keep, send = project(
        place, scalars, mixed, mixed_other, reward_dir[0], weight
    )
    parts = weight_gradient(place, mixed, mixed_other, grad_out)
    grad_h = over_seq(add_after(keep, swap_cfg(send), parts[4]))
    sums = scatter_pairs(parts)
    guided_all = joined(guided, swap_cfg(guided), first_core)
    grad_value_h = grad_of_value(grad_h, probs)
    grad_value = over_seq(grad_value_h)
    packed = attend_backward(first, value, mixed_h, grad_h, grad_value_h, probs)
    last = over_seq(fill_extra(*sums, packed, grad_value))
    grad_half = sum_extra(last, deep)
    grad_weight = joined(grad_half, swap_cfg(grad_half), first_core)
    (grad_value,) = unpack_heads(grad_value, 1, rows)
    grad_query, grad_key = unpack_heads(last, 2, rows)
    return (
        guided_all[None],
        grad_query[None, None],
        grad_key[None, None],
        grad_value[None, None],
        grad_weight,
    )


def solution(mesh):
    placed = (
        P("cfg", "fsdp", "seq", None),
        P("cfg", "fsdp", "seq", None),
        P("cfg", "fsdp", "seq", None),
        P(("fsdp", "seq"), None),
        P("fsdp", "seq", None),
        P(),
        P(),
    )
    return jax.shard_map(
        local,
        mesh=mesh,
        in_specs=placed,
        out_specs=(
            P("fsdp", "seq", None),
            P("cfg", "fsdp", "seq", None),
            P("cfg", "fsdp", "seq", None),
            P("cfg", "fsdp", "seq", None),
            P(("fsdp", "seq"), None),
        ),
        check_vma=False,
    )
```

```python
import functools

import jax
import jax.numpy as jnp
from jax import lax
from jax.experimental import pallas as pl
from jax.experimental.pallas import tpu as pltpu
from jax.sharding import PartitionSpec as P

HDIM = 128
STEPS = 50
GUIDE_STEP = 0.04
LOG2E = 1.4426950408889634
BF = jnp.bfloat16
F32 = jnp.float32
NT = (((1,), (1,)), ((), ()))
VMEM_LIMIT = 20 * 1024 * 1024
EXTRA = 48


def params():
    return pltpu.CompilerParams(vmem_limit_bytes=VMEM_LIMIT)


def whole(count):
    return [pl.BlockSpec(memory_space=pltpu.VMEM) for _ in range(count)]


def anywhere():
    return pl.BlockSpec(memory_space=pl.ANY)


def full(array):
    rank = len(array.shape)
    return pl.BlockSpec(array.shape, lambda i: (0,) * rank)


def scalars_spec():
    return pl.BlockSpec(memory_space=pltpu.SMEM)


def call(kernel, name, out_shape, in_specs, out_specs=None, **kwargs):
    if out_specs is None:
        out_specs = whole(len(out_shape)) if isinstance(out_shape, tuple) else whole(1)[0]
    return pl.pallas_call(
        kernel,
        out_shape=out_shape,
        in_specs=in_specs,
        out_specs=tuple(out_specs) if isinstance(out_shape, tuple) else out_specs,
        compiler_params=params(),
        cost_estimate=pl.CostEstimate(flops=1, bytes_accessed=1, transcendentals=0),
        name=name,
        **kwargs,
    )


def shaped(shape, dtype=BF):
    return jax.ShapeDtypeStruct(shape, dtype)


def kept(shape, dtype=BF):
    return pltpu.VMEM(shape, dtype)


def pin(array):
    return pltpu.with_memory_space_constraint(array, pltpu.VMEM)


def spilled(shape, dtype=BF):
    return pltpu.HBM(shape, dtype)


def out(array):
    return pltpu.with_memory_space_constraint(array, pltpu.HBM)


def ordered(orders):
    return [anywhere()] * len(orders)


def lanes_of(head):
    return slice(head * HDIM, (head + 1) * HDIM)


def pack_first_kernel(place_ref, q_ref, k_ref, w_ref, out_ref):
    rows = q_ref.shape[0]
    deep = w_ref.shape[0]
    first = place_ref[0] == 0
    half = w_ref.shape[1] // 2
    picked = jnp.where(first, w_ref[:, :half], w_ref[:, half:])
    heads = out_ref.shape[0]
    per = EXTRA // deep
    for head in range(heads):
        side = head // (heads // 2)
        for part in range(per):
            out_ref[head, part * deep : (part + 1) * deep, :] = picked[:, lanes_of(side * per + part)]
        out_ref[head, EXTRA : EXTRA + rows, :] = q_ref[:, lanes_of(head)]
        out_ref[head, EXTRA + rows :, :] = k_ref[:, lanes_of(head)]


def pack_first(place, query, key, weight):
    rows, width = query.shape
    return call(
        pack_first_kernel,
        "pack_first",
        kept((width // HDIM, EXTRA + 2 * rows, HDIM)),
        [scalars_spec(), full(query), full(key), full(weight)],
        grid=(1,),
    )(place, out(query), out(key), out(weight))


def pack_kernel(in_ref, out_ref):
    for head in range(out_ref.shape[0]):
        out_ref[head] = in_ref[:, lanes_of(head)]


def pack_heads(array):
    rows, width = array.shape
    return call(pack_kernel, "pack_heads", kept((width // HDIM, rows, HDIM)), [full(array)], grid=(1,))(
        out(array)
    )


def unpack_kernel(in_ref, order_ref, *out_refs):
    rows = out_refs[0].shape[0]
    skip = in_ref.shape[1] - rows * len(out_refs)
    for head in range(in_ref.shape[0]):
        for place, ref in enumerate(out_refs):
            start = skip + place * rows
            ref[:, lanes_of(head)] = in_ref[head, start : start + rows, :]


def unpack_heads(packed, count, rows, order):
    target = shaped((rows, packed.shape[0] * HDIM))
    specs = [full(packed), anywhere()]
    return call(
        unpack_kernel, "unpack_heads", (target,) * count, specs, [full(target)] * count, grid=(1,)
    )(packed, out(order))


def extra_spec(packed):
    return pl.BlockSpec((packed.shape[0], EXTRA, HDIM), lambda i: (0, 0, 0))


def piece_kernel(in_ref, out_ref):
    per = out_ref.shape[1] // HDIM
    deep = EXTRA // per
    for source in range(in_ref.shape[0]):
        for part in range(per):
            out_ref[source * deep : (source + 1) * deep, lanes_of(part)] = in_ref[
                source, part * deep : (part + 1) * deep, :
            ]


def weight_piece(packed, deep):
    return call(
        piece_kernel,
        "weight_piece",
        shaped((packed.shape[0] * deep, EXTRA // deep * HDIM)),
        [extra_spec(packed)],
        grid=(1,),
    )(packed)


CHUNK = 512


def probs_kernel(first_ref, order_ref, probs_ref, held, sems):
    shards, total_rows, _ = first_ref.shape
    rows = (total_rows - EXTRA) // 2
    length = shards * rows
    keys = first_ref[:, EXTRA + rows :, :].reshape(length, HDIM)
    scale = HDIM ** (-0.5) * LOG2E
    take = CHUNK // rows
    copies = []
    for part in range(length // CHUNK):
        here = slice(part * take, (part + 1) * take)
        query = first_ref[here, EXTRA : EXTRA + rows, :].reshape(CHUNK, HDIM)
        scores = lax.dot_general(keys, query, NT, preferred_element_type=F32)
        peak = jnp.max(scores, axis=0, keepdims=True) * scale
        weights = jnp.exp2(scores * scale - peak)
        total = jnp.sum(weights, axis=0, keepdims=True)
        lanes = pl.ds(part * CHUNK, CHUNK)
        held[:, lanes] = (weights * (1.0 / total)).astype(BF)
        copy = pltpu.make_async_copy(held.at[:, lanes], probs_ref.at[:, lanes], sems.at[part])
        copy.start()
        copies.append(copy)
    for copy in copies:
        copy.wait()


def probabilities(first, order):
    shards, total_rows, _ = first.shape
    length = shards * (total_rows - EXTRA) // 2
    return call(
        probs_kernel,
        "probabilities",
        spilled((length, length)),
        whole(1) + [anywhere()],
        anywhere(),
        scratch_shapes=[
            pltpu.VMEM((length, length), BF),
            pltpu.SemaphoreType.DMA((length // CHUNK,)),
        ],
    )(first, order)


def fetch(probs_ref, held, sems, by_rows):
    copies = []
    for part in range(sems.shape[0]):
        span = pl.ds(part * CHUNK, CHUNK)
        where = (span,) if by_rows else (slice(None), span)
        copies.append(pltpu.make_async_copy(probs_ref.at[where], held.at[where], sems.at[part]))
    for copy in copies:
        copy.start()
    return copies


def fetch_scratch(probs):
    return [pltpu.VMEM(probs.shape, BF), pltpu.SemaphoreType.DMA((probs.shape[0] // CHUNK,))]


def mix_kernel(value_ref, probs_ref, *refs):
    out_ref, held, sems = refs[-3:]
    copies = fetch(probs_ref, held, sems, False)
    shards, rows, _ = value_ref.shape
    length = shards * rows
    value_t = value_ref[...].reshape(length, HDIM).astype(F32).T.astype(BF)
    take = CHUNK // rows
    for part in range(length // CHUNK):
        copies[part].wait()
        lanes = slice(part * CHUNK, (part + 1) * CHUNK)
        mixed_t = jnp.dot(value_t, held[:, lanes], preferred_element_type=F32)
        out_ref[part * take : (part + 1) * take] = mixed_t.T.astype(BF).reshape(take, rows, HDIM)


def mix(value, probs, *orders):
    return call(
        mix_kernel,
        "mix",
        kept(value.shape),
        whole(1) + [anywhere()] + ordered(orders),
        scratch_shapes=fetch_scratch(probs),
    )(value, out(probs), *[out(order) for order in orders])


def grad_value_kernel(grad_ref, probs_ref, out_ref, held, sems):
    copies = fetch(probs_ref, held, sems, True)
    shards, rows, _ = grad_ref.shape
    length = shards * rows
    grad = grad_ref[...].reshape(length, HDIM)
    take = CHUNK // rows
    for part in range(length // CHUNK):
        copies[part].wait()
        span = slice(part * CHUNK, (part + 1) * CHUNK)
        result = jnp.dot(held[span, :], grad, preferred_element_type=F32)
        out_ref[part * take : (part + 1) * take] = result.astype(BF).reshape(take, rows, HDIM)


def grad_of_value(grad, probs):
    return call(
        grad_value_kernel,
        "grad_of_value",
        kept(grad.shape),
        whole(1) + [anywhere()],
        scratch_shapes=fetch_scratch(probs),
    )(grad, out(probs))


def backward_kernel(
    first_ref, value_ref, mixed_ref, grad_ref, probs_ref, order_ref, out_ref, query_t, held, sems
):
    copies = fetch(probs_ref, held, sems, True)
    shards, rows, _ = value_ref.shape
    length = shards * rows
    factor = HDIM ** (-0.5)
    grad = grad_ref[...].reshape(length, HDIM)
    mixed = mixed_ref[...].reshape(length, HDIM)
    product = grad.astype(F32) * mixed.astype(F32)
    inner = jnp.sum(product.T, axis=0, keepdims=True)
    query = first_ref[:, EXTRA : EXTRA + rows, :].reshape(length, HDIM)
    chunk = CHUNK // 2
    take = chunk // rows
    for part in range(length // chunk):
        if part % 2 == 0:
            copies[part // 2].wait()
        here = slice(part * take, (part + 1) * take)
        span = slice(part * chunk, (part + 1) * chunk)
        keys = first_ref[here, EXTRA + rows :, :].reshape(chunk, HDIM)
        value = value_ref[here].reshape(chunk, HDIM)
        grad_probs = lax.dot_general(value, grad, NT, preferred_element_type=F32)
        grad_scores = (held[span, :].astype(F32) * (grad_probs - inner)).astype(BF)
        grad_key = jnp.dot(grad_scores, query, preferred_element_type=F32) * factor
        out_ref[here, EXTRA + rows :, :] = grad_key.astype(BF).reshape(take, rows, HDIM)
        keys_t = keys.astype(F32).T.astype(BF)
        piece = jnp.dot(keys_t, grad_scores, preferred_element_type=F32)
        if part == 0:
            query_t[...] = piece
        else:
            query_t[...] += piece
    grad_query = (query_t[...] * factor).T.astype(BF)
    out_ref[:, EXTRA : EXTRA + rows, :] = grad_query.reshape(shards, rows, HDIM)
    out_ref[:, :EXTRA, :] = jnp.zeros((shards, EXTRA, HDIM), BF)


def attend_backward(first, value, mixed, grad, probs, order):
    length = value.shape[0] * value.shape[1]
    return call(
        backward_kernel,
        "attend_backward",
        kept(first.shape),
        [full(first), full(value), full(mixed), full(grad), anywhere(), anywhere()],
        grid=(1,),
        scratch_shapes=[pltpu.VMEM((HDIM, length), F32)] + fetch_scratch(probs),
    )(first, value, mixed, grad, out(probs), out(order))


def piece_place(place_ref, slot):
    block = place_ref[1 + 2 * slot]
    side = place_ref[2 + 2 * slot]
    return block, side


def piece_span(place_ref, slot, deep, wide):
    block, side = piece_place(place_ref, slot)
    rows = pl.ds(pl.multiple_of(block * deep, deep), deep)
    lanes = pl.ds(pl.multiple_of(side * wide, HDIM), wide)
    return rows, lanes


def assemble_kernel(place_ref, *refs):
    pairs, out_ref = refs[:8], refs[8]
    deep, wide = pairs[0].shape[1:]
    for slot in range(16):
        rows, lanes = piece_span(place_ref, slot, deep, wide)
        out_ref[rows, lanes] = pairs[slot // 2][slot % 2]


def assemble(place, pairs):
    _, deep, wide = pairs[0].shape
    return call(
        assemble_kernel,
        "assemble",
        kept((8 * deep, 2 * wide)),
        [scalars_spec()] + [full(pair) for pair in pairs],
        grid=(1,),
    )(place, *[out(pair) for pair in pairs])


def project_kernel(
    place_ref, scalar_ref, own_ref, other_ref, reward_ref, weight_ref,
    guided_ref, grad_ref, keep_ref, send_ref,
):
    rows = own_ref.shape[1]
    half = guided_ref.shape[1]
    heads = own_ref.shape[0]
    blocks = heads // 2
    deep = 2 * HDIM
    first = place_ref[0] == 0
    gate, strength = scalar_ref[0], scalar_ref[1]
    total = None
    for block in range(blocks):
        head = 2 * block
        columns = jnp.concatenate(
            [
                jnp.concatenate([own_ref[head], own_ref[head + 1]], axis=1),
                jnp.concatenate([other_ref[head], other_ref[head + 1]], axis=1),
            ],
            axis=0,
        )
        part = jnp.dot(
            columns, weight_ref[block * deep : (block + 1) * deep], preferred_element_type=F32
        )
        total = part if total is None else total + part
    branch_out = (gate * total).astype(BF).astype(F32)
    own_out, other_out = branch_out[:rows], branch_out[rows:]
    cond = jnp.where(first, own_out, other_out)
    uncond = jnp.where(first, other_out, own_out)
    guided = uncond + strength * (cond - uncond)
    guided_ref[...] = guided.astype(BF)
    reward = jnp.where(first, reward_ref[:, :half], reward_ref[:, half:]).astype(F32)
    resid = reward - guided
    own_coeff = gate * jnp.where(first, strength, 1.0 - strength)
    other_coeff = gate * jnp.where(first, 1.0 - strength, strength)
    grad = jnp.concatenate([own_coeff * resid, other_coeff * resid], axis=0).astype(BF)
    grad_ref[...] = grad
    for block in range(blocks):
        part = lax.dot_general(
            grad, weight_ref[block * deep : (block + 1) * deep], NT, preferred_element_type=F32
        )
        for odd in range(2):
            lanes = part[:, lanes_of(odd)]
            keep_ref[2 * block + odd] = lanes[:rows]
            send_ref[2 * block + odd] = lanes[rows:].astype(BF)


def project(place, scalars, own, other, reward, weight):
    heads, rows, _ = own.shape
    half = reward.shape[1] // 2
    return call(
        project_kernel,
        "project",
        (
            spilled((rows, half)),
            kept((2 * rows, half)),
            kept((heads, rows, HDIM), F32),
            kept((heads, rows, HDIM)),
        ),
        [scalars_spec(), scalars_spec()] + whole(2) + [full(reward)] + whole(1),
        [pl.BlockSpec((rows, half), lambda i: (0, 0))] + whole(3),
        grid=(1,),
    )(place, scalars, pin(own), pin(other), out(reward), pin(weight))


def weight_kernel(place_ref, own_ref, other_ref, grad_ref, *refs):
    pairs, held = refs[:8], refs[8]
    deep, wide = pairs[0].shape[1:]
    grad = grad_ref[...]
    for head in range(own_ref.shape[0]):
        flipped = jnp.concatenate([own_ref[head].T, other_ref[head].T], axis=1)
        part = jnp.dot(flipped, grad, preferred_element_type=F32)
        held[head * HDIM : (head + 1) * HDIM] = part.astype(BF)
    for slot in range(16):
        rows, lanes = piece_span(place_ref, slot, deep, wide)
        pairs[slot // 2][slot % 2] = held[rows, lanes]


def weight_gradient(place, own, other, grad):
    heads = own.shape[0]
    half = grad.shape[1]
    pair = spilled((2, 2 * HDIM, half // 2))
    return call(
        weight_kernel,
        "weight_gradient",
        (pair,) * 8,
        [scalars_spec()] + whole(3),
        [full(pair)] * 8,
        grid=(1,),
        scratch_shapes=[pltpu.VMEM((heads * HDIM, half), BF)],
    )(place, pin(own), pin(other), pin(grad))


def add_kernel(keep_ref, got_ref, order_ref, out_ref):
    out_ref[...] = (keep_ref[...] + got_ref[...].astype(F32)).astype(BF)


def add_after(keep, got, order):
    return call(add_kernel, "add_after", kept(got.shape), whole(2) + [anywhere()])(
        pin(keep), pin(got), out(order)
    )


def hold_kernel(in_ref, *refs):
    del refs


def hold(array, *orders):
    return call(
        hold_kernel,
        "hold",
        kept(array.shape),
        whole(1) + ordered(orders),
        input_output_aliases={0: 0},
    )(pin(array), *[out(order) for order in orders])


def fill_kernel(here_ref, left_ref, right_ref, far_ref, packed_ref, first_order, second_order, out_ref):
    per = here_ref.shape[1] // HDIM
    deep = EXTRA // per
    total = here_ref[...] + left_ref[...].astype(F32) + right_ref[...].astype(F32)
    total = (total + far_ref[...].astype(F32)).astype(BF)
    for target in range(out_ref.shape[0]):
        for part in range(per):
            out_ref[target, part * deep : (part + 1) * deep, :] = total[
                target * deep : (target + 1) * deep, lanes_of(part)
            ]


def fill_extra(here, left, right, far, packed, first_order, second_order):
    return call(
        fill_kernel,
        "fill_extra",
        kept(packed.shape),
        [full(array) for array in (here, left, right, far)] + whole(1) + [anywhere()] * 2,
        whole(1)[0],
        grid=(1,),
        input_output_aliases={4: 0},
    )(out(here), out(left), out(right), out(far), pin(packed), out(first_order), out(second_order))


def sum_kernel(in_ref, out_ref):
    sources = in_ref.shape[0]
    deep = out_ref.shape[0]
    per = EXTRA // deep
    for side in range(2):
        for part in range(per):
            rows = slice(part * deep, (part + 1) * deep)
            total = None
            for source in range(sources // 2):
                piece = in_ref[side * (sources // 2) + source, rows, :].astype(F32)
                total = piece if total is None else total + piece
            out_ref[:, lanes_of(side * per + part)] = total


def sum_extra(packed, deep):
    return call(
        sum_kernel,
        "sum_extra",
        shaped((deep, 2 * (EXTRA // deep) * HDIM), F32),
        [extra_spec(packed)],
        grid=(1,),
    )(packed)


def swap_cfg(value):
    return lax.ppermute(value, "cfg", [(0, 1), (1, 0)])


def shift_y(value, step):
    pairs = [(i, (i // 4) * 4 + (i % 4 + step) % 4) for i in range(8)]
    return lax.ppermute(value, "fsdp", pairs)


def shift_x(value, step):
    pairs = []
    for fsdp in range(8):
        for seq in range(16):
            x = ((fsdp // 4) * 2 + seq // 8 + step) % 4
            target = ((x // 2) * 4 + fsdp % 4) * 16 + (x % 2) * 8 + seq % 8
            pairs.append((fsdp * 16 + seq, target))
    return lax.ppermute(value, ("fsdp", "seq"), pairs)


def gather_pairs(piece):
    right, left, far = shift_x(piece, -1), shift_x(piece, 1), shift_x(piece, 2)
    near = jnp.stack([piece, right])
    past = jnp.stack([far, left])
    near_left, near_right = shift_y(near, 1), shift_y(near, -1)
    past_left, past_right = shift_y(past, 1), shift_y(past, -1)
    near_far = shift_y(near_left, 1)
    past_far = shift_y(past_right, -1)
    return (near, past, near_right, past_right, near_far, past_far, near_left, past_left)


def plus(one, two):
    return one[...].astype(F32) + two[...].astype(F32)


def pair_kernel(*refs):
    near, past, near_right, past_left, from_left, from_right, got_past, got_near = refs[:8]
    near_out, past_out, right_out, left_out = refs[9:]
    right_out[...] = plus(near_right, from_left).astype(BF)
    left_out[...] = plus(past_left, from_right).astype(BF)
    near_out[...] = plus(near, got_near)
    past_out[...] = plus(past, got_past)


def pair_sums(pairs, order):
    shape = pairs[0].shape
    outs = (spilled(shape, F32),) * 2 + (spilled(shape),) * 2
    return call(
        pair_kernel,
        "pair_sums",
        outs,
        [full(pair) for pair in pairs] + [anywhere()],
        [full(target) for target in outs],
        grid=(1,),
    )(*[out(pair) for pair in pairs], out(order))


def ring_kernel(near, near_got, past, past_got, here_ref, right_ref, far_ref, left_ref):
    outs = ((here_ref, right_ref), (far_ref, left_ref))
    for refs, targets in zip(((near, near_got), (past, past_got)), outs):
        for slot, target in enumerate(targets):
            target[...] = (refs[0][slot] + refs[1][slot].astype(F32)).astype(target.dtype)


def ring_sums(*pairs):
    shape = pairs[0].shape[1:]
    outs = (spilled(shape, F32),) + (spilled(shape),) * 3
    return call(
        ring_kernel,
        "ring_sums",
        outs,
        [full(pair) for pair in pairs],
        [full(target) for target in outs],
        grid=(1,),
    )(*[out(pair) for pair in pairs])


def scatter_y(parts, order):
    near, past, near_right, past_right, near_far, past_far, near_left, past_left = parts
    received = (
        shift_y(near_far, 1),
        shift_y(past_far, -1),
        shift_y(past_right, 1),
        shift_y(near_left, -1),
    )
    near, past, right, left = pair_sums((near, past, near_right, past_left) + received, order)
    return near, shift_y(right, 1), past, shift_y(left, -1)


def scatter_x(near, near_got, past, past_got):
    here, right, far, left = ring_sums(near, near_got, past, past_got)
    return here, shift_x(right, 1), shift_x(left, -1), shift_x(far, 2)


def over_seq(array):
    return lax.all_to_all(array, "seq", split_axis=0, concat_axis=0, tiled=True)


def join_kernel(place_ref, own_ref, other_ref, order_ref, out_ref):
    first = place_ref[0] == 0
    half = own_ref.shape[1]
    out_ref[:, :half] = jnp.where(first, own_ref[...], other_ref[...])
    out_ref[:, half:] = jnp.where(first, other_ref[...], own_ref[...])


def joined(place, own, other, order):
    rows, half = own.shape
    return call(
        join_kernel,
        "joined",
        shaped((rows, 2 * half), own.dtype),
        [scalars_spec(), full(own), full(other), anywhere()],
        pl.BlockSpec((rows, 2 * half), lambda i: (0, 0)),
        grid=(1,),
    )(place, out(own), out(other), out(order))


def places():
    cfg = lax.axis_index("cfg")
    fsdp = lax.axis_index("fsdp")
    x = (fsdp >> 2) * 2 + (lax.axis_index("seq") >> 3)
    y = fsdp & 3
    slots = jnp.arange(16)
    there = (x + (slots & 3)) & 3
    block = (there >> 1) * 4 + ((y + (slots >> 2)) & 3)
    table = jnp.stack([block, there & 1], axis=1).reshape(-1)
    return jnp.concatenate([cfg[None], table]).astype(jnp.int32)


def local(query_act, key_act, value_act, out_weight, reward_dir, guide_index, step_index):
    place = places()
    moment = step_index[0].astype(F32)
    gate = jnp.cos(0.5 * jnp.pi * (moment + 0.5) / STEPS)
    strength = 1.0 + GUIDE_STEP * guide_index[0].astype(F32)
    scalars = jnp.stack([gate, strength])
    deep = out_weight.shape[0]
    rows = query_act.shape[2]

    first = over_seq(pack_first(place, query_act[0, 0], key_act[0, 0], out_weight))
    value = over_seq(pack_heads(value_act[0, 0]))
    piece = weight_piece(first, deep)
    pairs = gather_pairs(piece)
    weight = assemble(place, pairs)
    probs = probabilities(first, piece)
    mixed_h = mix(value, probs, pairs[1], pairs[2], pairs[6])
    mixed = hold(over_seq(mixed_h), pairs[3], pairs[4], pairs[5], pairs[7])
    mixed_other = swap_cfg(mixed)
    guided, grad_out, keep, send = project(
        place, scalars, mixed, mixed_other, reward_dir[0], weight
    )
    parts = weight_gradient(place, mixed, mixed_other, grad_out)
    grad_mixed = add_after(keep, swap_cfg(send), parts[4])
    grad_h = over_seq(grad_mixed)
    grad_value_h = grad_of_value(grad_h, probs)
    grad_value = over_seq(grad_value_h)
    ring = scatter_y(parts, grad_value_h)
    guided_all = joined(place, guided, swap_cfg(guided), grad_value_h)
    packed = attend_backward(first, value, mixed_h, grad_h, probs, grad_value_h)
    last = over_seq(fill_extra(*scatter_x(*ring), packed, grad_value, guided_all))
    grad_half = sum_extra(last, deep)
    grad_weight = joined(place, grad_half, swap_cfg(grad_half), grad_half)
    (grad_value,) = unpack_heads(grad_value, 1, rows, place)
    grad_query, grad_key = unpack_heads(last, 2, rows, grad_value)
    return (
        guided_all[None],
        grad_query[None, None],
        grad_key[None, None],
        grad_value[None, None],
        grad_weight,
    )


def solution(mesh):
    placed = (
        P("cfg", "fsdp", "seq", None),
        P("cfg", "fsdp", "seq", None),
        P("cfg", "fsdp", "seq", None),
        P(("fsdp", "seq"), None),
        P("fsdp", "seq", None),
        P(),
        P(),
    )
    return jax.shard_map(
        local,
        mesh=mesh,
        in_specs=placed,
        out_specs=(
            P("fsdp", "seq", None),
            P("cfg", "fsdp", "seq", None),
            P("cfg", "fsdp", "seq", None),
            P("cfg", "fsdp", "seq", None),
            P(("fsdp", "seq"), None),
        ),
        check_vma=False,
    )
```

```python
import functools

import jax
import jax.numpy as jnp
from jax import lax
from jax.experimental import pallas as pl
from jax.experimental.pallas import tpu as pltpu
from jax.sharding import PartitionSpec as P

HDIM = 128
STEPS = 50
GUIDE_STEP = 0.04
LOG2E = 1.4426950408889634
BF = jnp.bfloat16
F32 = jnp.float32
NT = (((1,), (1,)), ((), ()))
VMEM_LIMIT = 20 * 1024 * 1024


def params():
    return pltpu.CompilerParams(vmem_limit_bytes=VMEM_LIMIT)


def whole(count):
    return [pl.BlockSpec(memory_space=pltpu.VMEM) for _ in range(count)]


def anywhere():
    return pl.BlockSpec(memory_space=pl.ANY)


def full(array):
    rank = len(array.shape)
    return pl.BlockSpec(array.shape, lambda i: (0,) * rank)


def scalars_spec():
    return pl.BlockSpec(memory_space=pltpu.SMEM)


def call(kernel, name, out_shape, in_specs, out_specs=None, flops=1, **kwargs):
    if out_specs is None:
        out_specs = whole(len(out_shape)) if isinstance(out_shape, tuple) else whole(1)[0]
    return pl.pallas_call(
        kernel,
        out_shape=out_shape,
        in_specs=in_specs,
        out_specs=tuple(out_specs) if isinstance(out_shape, tuple) else out_specs,
        compiler_params=params(),
        cost_estimate=pl.CostEstimate(flops=flops, bytes_accessed=1, transcendentals=0),
        name=name,
        **kwargs,
    )


def shaped(shape, dtype=BF):
    return jax.ShapeDtypeStruct(shape, dtype)


def kept(shape, dtype=BF):
    return pltpu.VMEM(shape, dtype)


def pin(array):
    return pltpu.with_memory_space_constraint(array, pltpu.VMEM)


def spilled(shape, dtype=BF):
    return pltpu.HBM(shape, dtype)


def out(array):
    return pltpu.with_memory_space_constraint(array, pltpu.HBM)


def ordered(orders):
    return [anywhere()] * len(orders)


def lanes_of(head):
    return slice(head * HDIM, (head + 1) * HDIM)


def pack_kernel(*refs):
    in_refs, out_ref = refs[:-1], refs[-1]
    rows = in_refs[0].shape[0]
    for head in range(out_ref.shape[0]):
        for place, ref in enumerate(in_refs):
            out_ref[head, place * rows : (place + 1) * rows, :] = ref[:, lanes_of(head)]


def pack_heads(*arrays):
    rows, width = arrays[0].shape
    return call(
        pack_kernel,
        "pack_heads",
        kept((width // HDIM, len(arrays) * rows, HDIM)),
        [full(array) for array in arrays],
        grid=(1,),
    )(*[out(array) for array in arrays])


def unpack_kernel(in_ref, *out_refs):
    rows = out_refs[0].shape[0]
    for head in range(in_ref.shape[0]):
        for place, ref in enumerate(out_refs):
            ref[:, lanes_of(head)] = in_ref[head, place * rows : (place + 1) * rows, :]


def unpack_heads(packed, count):
    target = shaped((packed.shape[1] // count, packed.shape[0] * HDIM))
    return call(
        unpack_kernel,
        "unpack_heads",
        (target,) * count,
        [full(packed)],
        [full(target)] * count,
        grid=(1,),
    )(packed)


CHUNK = 512


def forward_kernel(qkv_ref, *refs):
    out_ref, probs_ref, held, sems = refs[-4:]
    shards, total_rows, _ = qkv_ref.shape
    rows = total_rows // 3
    length = shards * rows
    keys = qkv_ref[:, rows : 2 * rows, :].reshape(length, HDIM)
    value_t = qkv_ref[:, 2 * rows :, :].reshape(length, HDIM).astype(F32).T.astype(BF)
    scale = HDIM ** (-0.5) * LOG2E
    take = CHUNK // rows
    copies = []
    for part in range(length // CHUNK):
        here = slice(part * take, (part + 1) * take)
        query = qkv_ref[here, :rows, :].reshape(CHUNK, HDIM)
        scores = lax.dot_general(keys, query, NT, preferred_element_type=F32)
        peak = jnp.max(scores, axis=0, keepdims=True) * scale
        weights = jnp.exp2(scores * scale - peak)
        total = jnp.sum(weights, axis=0, keepdims=True)
        probs = (weights * (1.0 / total)).astype(BF)
        lanes = pl.ds(part * CHUNK, CHUNK)
        held[:, lanes] = probs
        copy = pltpu.make_async_copy(held.at[:, lanes], probs_ref.at[:, lanes], sems.at[part])
        copy.start()
        copies.append(copy)
        mixed_t = jnp.dot(value_t, probs, preferred_element_type=F32)
        out_ref[here] = mixed_t.T.astype(BF).reshape(take, rows, HDIM)
    for copy in copies:
        copy.wait()


def attend_forward(qkv, *orders):
    shards, total_rows, _ = qkv.shape
    rows = total_rows // 3
    length = shards * rows
    return call(
        forward_kernel,
        "attend_forward",
        (kept((shards, rows, HDIM)), spilled((length, length))),
        whole(1) + ordered(orders),
        whole(1) + [anywhere()],
        scratch_shapes=[
            pltpu.VMEM((length, length), BF),
            pltpu.SemaphoreType.DMA((length // CHUNK,)),
        ],
    )(qkv, *[out(order) for order in orders])


def backward_kernel(qkv_ref, mixed_ref, grad_ref, probs_ref, *refs):
    out_ref, query_t, held, sems = refs[-4:]
    copies = []
    for part in range(sems.shape[0]):
        span = pl.ds(part * CHUNK, CHUNK)
        copies.append(pltpu.make_async_copy(probs_ref.at[span], held.at[span], sems.at[part]))
    for copy in copies:
        copy.start()
    shards, rows, _ = mixed_ref.shape
    length = shards * rows
    factor = HDIM ** (-0.5)
    grad = grad_ref[...].reshape(length, HDIM)
    mixed = mixed_ref[...].reshape(length, HDIM)
    product = grad.astype(F32) * mixed.astype(F32)
    inner = jnp.sum(product.T, axis=0, keepdims=True)
    query = qkv_ref[:, :rows, :].reshape(length, HDIM)
    chunk = CHUNK // 2
    take = chunk // rows
    for part in range(length // chunk):
        if part % 2 == 0:
            copies[part // 2].wait()
        here = slice(part * take, (part + 1) * take)
        probs = held[part * chunk : (part + 1) * chunk, :]
        keys = qkv_ref[here, rows : 2 * rows, :].reshape(chunk, HDIM)
        value = qkv_ref[here, 2 * rows :, :].reshape(chunk, HDIM)
        grad_value = jnp.dot(probs, grad, preferred_element_type=F32)
        out_ref[here, 2 * rows :, :] = grad_value.astype(BF).reshape(take, rows, HDIM)
        grad_probs = lax.dot_general(value, grad, NT, preferred_element_type=F32)
        grad_scores = (probs.astype(F32) * (grad_probs - inner)).astype(BF)
        grad_key = jnp.dot(grad_scores, query, preferred_element_type=F32) * factor
        out_ref[here, rows : 2 * rows, :] = grad_key.astype(BF).reshape(take, rows, HDIM)
        keys_t = keys.astype(F32).T.astype(BF)
        piece = jnp.dot(keys_t, grad_scores, preferred_element_type=F32)
        if part == 0:
            query_t[...] = piece
        else:
            query_t[...] += piece
    grad_query = (query_t[...] * factor).T.astype(BF)
    out_ref[:, :rows, :] = grad_query.reshape(shards, rows, HDIM)


def attend_backward(qkv, mixed, grad, probs, *orders):
    length = probs.shape[0]
    return call(
        backward_kernel,
        "attend_backward",
        kept(qkv.shape),
        [full(qkv), full(mixed), full(grad), anywhere()] + ordered(orders),
        whole(1)[0],
        grid=(1,),
        flops=16 * length * length * HDIM,
        scratch_shapes=[
            pltpu.VMEM((HDIM, length), F32),
            pltpu.VMEM((length, length), BF),
            pltpu.SemaphoreType.DMA((length // CHUNK,)),
        ],
    )(out(qkv), out(mixed), grad, out(probs), *[out(order) for order in orders])


def head_of(place_ref, dx, dy):
    return place_ref[1 + 4 * dy + dx]


def assemble_kernel(place_ref, *refs):
    by_x, by_y, out_ref = refs[:4], refs[4:8], refs[-1]
    deep, wide = by_x[0].shape[1:]
    for dx in range(4):
        for dy in range(4):
            start = pl.multiple_of(head_of(place_ref, dx, dy) * deep, deep)
            out_ref[pl.ds(start, deep), :wide] = by_x[dx][dy]
            out_ref[pl.ds(start, deep), wide:] = by_y[dy][dx]


def assemble(place, groups, order):
    _, deep, wide = groups[0].shape
    return call(
        assemble_kernel,
        "assemble",
        kept((16 * deep, 2 * wide)),
        [scalars_spec()] + [full(group) for group in groups] + [anywhere()],
        whole(1)[0],
        grid=(1,),
    )(place, *[out(group) for group in groups], order)


def project_kernel(
    place_ref, scalar_ref, own_ref, other_ref, reward_ref, weight_ref,
    guided_ref, grad_ref, keep_ref, send_ref,
):
    rows = own_ref.shape[1]
    half = guided_ref.shape[1]
    heads = own_ref.shape[0]
    blocks = heads // 2
    deep = 2 * HDIM
    first = place_ref[0] == 0
    gate, strength = scalar_ref[0], scalar_ref[1]
    total = None
    for block in range(blocks):
        head = 2 * block
        columns = jnp.concatenate(
            [
                jnp.concatenate([own_ref[head], own_ref[head + 1]], axis=1),
                jnp.concatenate([other_ref[head], other_ref[head + 1]], axis=1),
            ],
            axis=0,
        )
        part = jnp.dot(
            columns, weight_ref[block * deep : (block + 1) * deep], preferred_element_type=F32
        )
        total = part if total is None else total + part
    branch_out = (gate * total).astype(BF).astype(F32)
    own_out, other_out = branch_out[:rows], branch_out[rows:]
    cond = jnp.where(first, own_out, other_out)
    uncond = jnp.where(first, other_out, own_out)
    guided = uncond + strength * (cond - uncond)
    guided_ref[...] = guided.astype(BF)
    reward = jnp.where(first, reward_ref[:, :half], reward_ref[:, half:]).astype(F32)
    resid = reward - guided
    own_coeff = gate * jnp.where(first, strength, 1.0 - strength)
    other_coeff = gate * jnp.where(first, 1.0 - strength, strength)
    grad = jnp.concatenate([own_coeff * resid, other_coeff * resid], axis=0).astype(BF)
    grad_ref[...] = grad
    for block in range(blocks):
        part = lax.dot_general(
            grad, weight_ref[block * deep : (block + 1) * deep], NT, preferred_element_type=F32
        )
        for odd in range(2):
            lanes = part[:, lanes_of(odd)]
            keep_ref[2 * block + odd] = lanes[:rows]
            send_ref[2 * block + odd] = lanes[rows:].astype(BF)


def project(place, scalars, own, other, reward, weight):
    heads, rows, _ = own.shape
    half = reward.shape[1] // 2
    return call(
        project_kernel,
        "project",
        (
            spilled((rows, half)),
            kept((2 * rows, half)),
            kept((heads, rows, HDIM), F32),
            kept((heads, rows, HDIM)),
        ),
        [scalars_spec(), scalars_spec()] + whole(2) + [full(reward)] + whole(1),
        [pl.BlockSpec((rows, half), lambda i: (0, 0))] + whole(3),
        grid=(1,),
    )(place, scalars, pin(own), pin(other), out(reward), pin(weight))


def weight_kernel(place_ref, own_ref, other_ref, grad_ref, order_ref, *refs):
    by_y, by_x = refs[:4], refs[4:]
    wide = by_x[0].shape[2]
    grad = grad_ref[...]
    for dx in range(4):
        for dy in range(4):
            head = head_of(place_ref, dx, dy)
            flipped = jnp.concatenate([own_ref[head].T, other_ref[head].T], axis=1)
            part = jnp.dot(flipped, grad, preferred_element_type=F32).astype(BF)
            by_y[dy][dx] = part[:, :wide]
            by_x[dx][dy] = part[:, wide:]


def weight_gradient(place, own, other, grad, order):
    group = spilled((4, HDIM, grad.shape[1] // 2))
    return call(
        weight_kernel,
        "weight_gradient",
        (group,) * 8,
        [scalars_spec()] + whole(3) + [anywhere()],
        [full(group)] * 8,
        grid=(1,),
    )(place, pin(own), pin(other), pin(grad), order)


def add_kernel(keep_ref, got_ref, out_ref):
    out_ref[...] = (keep_ref[...] + got_ref[...].astype(F32)).astype(BF)


def add_after(keep, got):
    return call(add_kernel, "add_after", kept(got.shape), whole(2))(pin(keep), pin(got))


def slices_kernel(place_ref, *refs):
    first, second, out_refs, held = refs[:4], refs[4:8], refs[8:-1], refs[-1]
    deep = out_refs[0].shape[0]
    wide = first[0].shape[1]
    held[:, :wide] = sum(ref[...].astype(F32) for ref in first)
    held[:, wide:] = sum(ref[...].astype(F32) for ref in second)
    for step, ref in enumerate(out_refs):
        start = pl.multiple_of(((place_ref[17] + step) & 7) * deep, deep)
        ref[...] = held[pl.ds(start, deep), :].astype(ref.dtype)


def z_slices(place, arrays):
    rows, wide = arrays[0].shape
    target = spilled((rows // 8, 2 * wide))
    return call(
        slices_kernel,
        "z_slices",
        (target,) * 8,
        [scalars_spec()] + [full(array) for array in arrays],
        [full(target)] * 8,
        grid=(1,),
        scratch_shapes=[pltpu.VMEM((rows, 2 * wide), F32)],
    )(place, *[out(array) for array in arrays])


def total_kernel(*refs):
    in_refs, out_ref = refs[:-2], refs[-1]
    total = in_refs[0][...].astype(F32)
    for ref in in_refs[1:]:
        total = total + ref[...].astype(F32)
    out_ref[...] = total


def total_of(arrays, order):
    return call(
        total_kernel,
        "total_of",
        kept(arrays[0].shape, F32),
        [full(array) for array in arrays] + [anywhere()],
        whole(1)[0],
        grid=(1,),
    )(*arrays, out(order))


def swap_cfg(value):
    return lax.ppermute(value, "cfg", [(0, 1), (1, 0)])


def shift_y(value, step):
    pairs = [(i, (i // 4) * 4 + (i % 4 + step) % 4) for i in range(8)]
    return lax.ppermute(value, "fsdp", pairs)


def shift_x(value, step):
    pairs = []
    for fsdp in range(8):
        for seq in range(16):
            x = ((fsdp // 4) * 2 + seq // 8 + step) % 4
            target = ((x // 2) * 4 + fsdp % 4) * 16 + (x % 2) * 8 + seq % 8
            pairs.append((fsdp * 16 + seq, target))
    return lax.ppermute(value, ("fsdp", "seq"), pairs)


def gather_groups(piece):
    half = piece.shape[1] // 2
    first, second = piece[:, :half], piece[:, half:]
    column = jnp.stack([first] + [shift_y(first, -step) for step in range(1, 4)])
    row = jnp.stack([second] + [shift_x(second, -step) for step in range(1, 4)])
    by_x = [column] + [shift_x(column, -step) for step in range(1, 4)]
    by_y = [row] + [shift_y(row, -step) for step in range(1, 4)]
    return by_x + by_y


def group_kernel(*refs):
    in_refs, out_refs = refs[:8], refs[8:]
    for side in range(2):
        for slot in range(4):
            total = sum(ref[slot].astype(F32) for ref in in_refs[4 * side : 4 * side + 4])
            target = out_refs[4 * side + slot]
            target[...] = total.astype(target.dtype)


def group_sums(groups):
    shape = groups[0].shape[1:]
    outs = ((spilled(shape, F32),) + (spilled(shape),) * 3) * 2
    return call(
        group_kernel,
        "group_sums",
        outs,
        [full(group) for group in groups],
        [full(target) for target in outs],
        grid=(1,),
    )(*[out(group) for group in groups])


def scatter_first(groups):
    by_y, by_x = groups[:4], groups[4:]
    first = [by_y[0]] + [shift_y(by_y[step], step) for step in range(1, 4)]
    second = [by_x[0]] + [shift_x(by_x[step], step) for step in range(1, 4)]
    return first + second


def scatter_rest(place, groups, order):
    sums = group_sums(groups)
    first = [sums[0]] + [shift_x(sums[step], step) for step in range(1, 4)]
    second = [sums[4]] + [shift_y(sums[4 + step], step) for step in range(1, 4)]
    slices = z_slices(place, first + second)
    parts = [slices[0]]
    for step in range(1, 8):
        pairs = [(i, (i & 8) + ((i + step) & 7)) for i in range(16)]
        parts.append(lax.ppermute(slices[step], "seq", pairs))
    return total_of(parts, order)


def over_seq(array):
    return lax.all_to_all(array, "seq", split_axis=0, concat_axis=0, tiled=True)


def over_z(array):
    groups = [list(range(8)), list(range(8, 16))]
    return lax.all_to_all(
        array, "seq", split_axis=0, concat_axis=0, axis_index_groups=groups, tiled=True
    )


def join_kernel(place_ref, own_ref, other_ref, order_ref, out_ref):
    first = place_ref[0] == 0
    half = own_ref.shape[1]
    out_ref[:, :half] = jnp.where(first, own_ref[...], other_ref[...])
    out_ref[:, half:] = jnp.where(first, other_ref[...], own_ref[...])


def joined(place, own, other, order, where=out):
    rows, half = own.shape
    return call(
        join_kernel,
        "joined",
        shaped((rows, 2 * half), own.dtype),
        [scalars_spec(), full(own), full(other), anywhere()],
        pl.BlockSpec((rows, 2 * half), lambda i: (0, 0)),
        grid=(1,),
    )(place, where(own), where(other), out(order))


def places():
    cfg = lax.axis_index("cfg")
    fsdp = lax.axis_index("fsdp")
    x = (fsdp >> 2) * 2 + (lax.axis_index("seq") >> 3)
    y = fsdp & 3
    slots = jnp.arange(16)
    there = (x + (slots & 3)) & 3
    block = (there >> 1) * 4 + ((y + (slots >> 2)) & 3)
    table = 2 * block + (there & 1)
    return jnp.concatenate([cfg[None], table, (lax.axis_index("seq") & 7)[None]]).astype(jnp.int32)


def local(query_act, key_act, value_act, out_weight, reward_dir, guide_index, step_index):
    place = places()
    moment = step_index[0].astype(F32)
    gate = jnp.cos(0.5 * jnp.pi * (moment + 0.5) / STEPS)
    strength = 1.0 + GUIDE_STEP * guide_index[0].astype(F32)
    scalars = jnp.stack([gate, strength])
    half = out_weight.shape[1] // 2
    own_half = jnp.where(place[0] == 0, out_weight[:, :half], out_weight[:, half:])
    piece = over_z(jnp.broadcast_to(own_half[None], (8,) + own_half.shape)).reshape(-1, half)
    groups = gather_groups(piece)
    qkv = over_seq(pack_heads(query_act[0, 0], key_act[0, 0], value_act[0, 0]))
    mixed_h, probs = attend_forward(qkv, *groups)
    mixed = over_seq(mixed_h)
    weight = assemble(place, groups, mixed)
    mixed_other = swap_cfg(mixed)
    guided, grad_out, keep, send = project(
        place, scalars, mixed, mixed_other, reward_dir[0], weight
    )
    grad_mixed = add_after(keep, swap_cfg(send))
    parts = weight_gradient(place, mixed, mixed_other, grad_out, grad_mixed)
    grad_h = over_seq(grad_mixed)
    parts = scatter_first(parts)
    packed = attend_backward(qkv, mixed_h, grad_h, probs, parts[0], parts[1], parts[5])
    guided_all = joined(place, guided, swap_cfg(guided), packed)
    last = over_seq(packed)
    grad_half = scatter_rest(place, parts, guided_all)
    grad_query, grad_key, grad_value = unpack_heads(last, 3)
    grad_weight = joined(place, grad_half, swap_cfg(grad_half), grad_query, pin)
    return (
        guided_all[None],
        grad_query[None, None],
        grad_key[None, None],
        grad_value[None, None],
        grad_weight,
    )


def solution(mesh):
    placed = (
        P("cfg", "fsdp", "seq", None),
        P("cfg", "fsdp", "seq", None),
        P("cfg", "fsdp", "seq", None),
        P(("fsdp", "seq"), None),
        P("fsdp", "seq", None),
        P(),
        P(),
    )
    return jax.shard_map(
        local,
        mesh=mesh,
        in_specs=placed,
        out_specs=(
            P("fsdp", "seq", None),
            P("cfg", "fsdp", "seq", None),
            P("cfg", "fsdp", "seq", None),
            P("cfg", "fsdp", "seq", None),
            P(("fsdp", "seq"), None),
        ),
        check_vma=False,
    )
```

```python
import functools

import jax
import jax.numpy as jnp
from jax import lax
from jax.experimental import pallas as pl
from jax.experimental.pallas import tpu as pltpu
from jax.sharding import PartitionSpec as P

HDIM = 128
STEPS = 50
GUIDE_STEP = 0.04
LOG2E = 1.4426950408889634
BF = jnp.bfloat16
F32 = jnp.float32
NT = (((1,), (1,)), ((), ()))
VMEM_LIMIT = 20 * 1024 * 1024


def params():
    return pltpu.CompilerParams(vmem_limit_bytes=VMEM_LIMIT)


def whole(count):
    return [pl.BlockSpec(memory_space=pltpu.VMEM) for _ in range(count)]


def anywhere():
    return pl.BlockSpec(memory_space=pl.ANY)


def full(array):
    rank = len(array.shape)
    return pl.BlockSpec(array.shape, lambda i: (0,) * rank)


def scalars_spec():
    return pl.BlockSpec(memory_space=pltpu.SMEM)


def call(kernel, name, out_shape, in_specs, out_specs=None, flops=1, **kwargs):
    if out_specs is None:
        out_specs = whole(len(out_shape)) if isinstance(out_shape, tuple) else whole(1)[0]
    return pl.pallas_call(
        kernel,
        out_shape=out_shape,
        in_specs=in_specs,
        out_specs=tuple(out_specs) if isinstance(out_shape, tuple) else out_specs,
        compiler_params=params(),
        cost_estimate=pl.CostEstimate(flops=flops, bytes_accessed=1, transcendentals=0),
        name=name,
        **kwargs,
    )


def shaped(shape, dtype=BF):
    return jax.ShapeDtypeStruct(shape, dtype)


def kept(shape, dtype=BF):
    return pltpu.VMEM(shape, dtype)


def pin(array):
    return pltpu.with_memory_space_constraint(array, pltpu.VMEM)


def spilled(shape, dtype=BF):
    return pltpu.HBM(shape, dtype)


def out(array):
    return pltpu.with_memory_space_constraint(array, pltpu.HBM)


def ordered(orders):
    return [anywhere()] * len(orders)


def lanes_of(head):
    return slice(head * HDIM, (head + 1) * HDIM)


def pack_kernel(*refs):
    in_refs, out_ref = refs[:-1], refs[-1]
    rows = in_refs[0].shape[0]
    for head in range(out_ref.shape[0]):
        for place, ref in enumerate(in_refs):
            out_ref[head, place * rows : (place + 1) * rows, :] = ref[:, lanes_of(head)]


def pack_heads(*arrays):
    rows, width = arrays[0].shape
    return call(
        pack_kernel,
        "pack_heads",
        kept((width // HDIM, len(arrays) * rows, HDIM)),
        [full(array) for array in arrays],
        grid=(1,),
    )(*[out(array) for array in arrays])


def unpack_kernel(in_ref, *out_refs):
    rows = out_refs[0].shape[0]
    for head in range(in_ref.shape[0]):
        for place, ref in enumerate(out_refs):
            ref[:, lanes_of(head)] = in_ref[head, place * rows : (place + 1) * rows, :]


def unpack_heads(packed, count):
    target = shaped((packed.shape[1] // count, packed.shape[0] * HDIM))
    return call(
        unpack_kernel,
        "unpack_heads",
        (target,) * count,
        [full(packed)],
        [full(target)] * count,
        grid=(1,),
    )(packed)


CHUNK = 512


def forward_kernel(qkv_ref, *refs):
    out_ref, probs_ref, held, sems = refs[-4:]
    shards, total_rows, _ = qkv_ref.shape
    rows = total_rows // 3
    length = shards * rows
    keys = qkv_ref[:, rows : 2 * rows, :].reshape(length, HDIM)
    value_t = qkv_ref[:, 2 * rows :, :].reshape(length, HDIM).astype(F32).T.astype(BF)
    scale = HDIM ** (-0.5) * LOG2E
    take = CHUNK // rows
    copies = []
    for part in range(length // CHUNK):
        here = slice(part * take, (part + 1) * take)
        query = qkv_ref[here, :rows, :].reshape(CHUNK, HDIM)
        scores = lax.dot_general(keys, query, NT, preferred_element_type=F32)
        peak = jnp.max(scores, axis=0, keepdims=True) * scale
        weights = jnp.exp2(scores * scale - peak)
        total = jnp.sum(weights, axis=0, keepdims=True)
        probs = (weights * (1.0 / total)).astype(BF)
        lanes = pl.ds(part * CHUNK, CHUNK)
        held[:, lanes] = probs
        copy = pltpu.make_async_copy(held.at[:, lanes], probs_ref.at[:, lanes], sems.at[part])
        copy.start()
        copies.append(copy)
        mixed_t = jnp.dot(value_t, probs, preferred_element_type=F32)
        out_ref[here] = mixed_t.T.astype(BF).reshape(take, rows, HDIM)
    for copy in copies:
        copy.wait()


def attend_forward(qkv, *orders):
    shards, total_rows, _ = qkv.shape
    rows = total_rows // 3
    length = shards * rows
    return call(
        forward_kernel,
        "attend_forward",
        (kept((shards, rows, HDIM)), spilled((length, length))),
        whole(1) + ordered(orders),
        whole(1) + [anywhere()],
        scratch_shapes=[
            pltpu.VMEM((length, length), BF),
            pltpu.SemaphoreType.DMA((length // CHUNK,)),
        ],
    )(qkv, *[out(order) for order in orders])


def backward_kernel(qkv_ref, mixed_ref, grad_ref, probs_ref, *refs):
    out_ref, query_t, held, sems = refs[-4:]
    copies = []
    for part in range(sems.shape[0]):
        span = pl.ds(part * CHUNK, CHUNK)
        copies.append(pltpu.make_async_copy(probs_ref.at[span], held.at[span], sems.at[part]))
    for copy in copies:
        copy.start()
    shards, rows, _ = mixed_ref.shape
    length = shards * rows
    factor = HDIM ** (-0.5)
    grad = grad_ref[...].reshape(length, HDIM)
    mixed = mixed_ref[...].reshape(length, HDIM)
    product = grad.astype(F32) * mixed.astype(F32)
    inner = jnp.sum(product.T, axis=0, keepdims=True)
    query = qkv_ref[:, :rows, :].reshape(length, HDIM)
    chunk = CHUNK // 2
    take = chunk // rows
    for part in range(length // chunk):
        if part % 2 == 0:
            copies[part // 2].wait()
        here = slice(part * take, (part + 1) * take)
        probs = held[part * chunk : (part + 1) * chunk, :]
        keys = qkv_ref[here, rows : 2 * rows, :].reshape(chunk, HDIM)
        value = qkv_ref[here, 2 * rows :, :].reshape(chunk, HDIM)
        grad_value = jnp.dot(probs, grad, preferred_element_type=F32)
        out_ref[here, 2 * rows :, :] = grad_value.astype(BF).reshape(take, rows, HDIM)
        grad_probs = lax.dot_general(value, grad, NT, preferred_element_type=F32)
        grad_scores = (probs.astype(F32) * (grad_probs - inner)).astype(BF)
        grad_key = jnp.dot(grad_scores, query, preferred_element_type=F32) * factor
        out_ref[here, rows : 2 * rows, :] = grad_key.astype(BF).reshape(take, rows, HDIM)
        keys_t = keys.astype(F32).T.astype(BF)
        piece = jnp.dot(keys_t, grad_scores, preferred_element_type=F32)
        if part == 0:
            query_t[...] = piece
        else:
            query_t[...] += piece
    grad_query = (query_t[...] * factor).T.astype(BF)
    out_ref[:, :rows, :] = grad_query.reshape(shards, rows, HDIM)


def attend_backward(qkv, mixed, grad, probs, *orders):
    length = probs.shape[0]
    return call(
        backward_kernel,
        "attend_backward",
        kept(qkv.shape),
        [full(qkv), full(mixed), full(grad), anywhere()] + ordered(orders),
        whole(1)[0],
        grid=(1,),
        flops=16 * length * length * HDIM,
        scratch_shapes=[
            pltpu.VMEM((HDIM, length), F32),
            pltpu.VMEM((length, length), BF),
            pltpu.SemaphoreType.DMA((length // CHUNK,)),
        ],
    )(out(qkv), out(mixed), grad, out(probs), *[out(order) for order in orders])


def head_of(place_ref, dx, dy):
    return place_ref[1 + 4 * dy + dx]


def head_of(place_ref, dx, dy):
    return place_ref[1 + 4 * dy + dx]


def assemble_kernel(place_ref, *refs):
    groups, out_ref = refs[:-2], refs[-1]
    deep = groups[0].shape[1]
    for dy, (one, two) in enumerate(zip(groups[:4], groups[4:])):
        for dx in range(4):
            start = pl.multiple_of(head_of(place_ref, dx, dy) * deep, deep)
            out_ref[pl.ds(start, deep), :] = (one if dx < 2 else two)[dx % 2]


def assemble(place, groups, order):
    _, deep, wide = groups[0].shape
    return call(
        assemble_kernel,
        "assemble",
        kept((16 * deep, wide)),
        [scalars_spec()] + [full(group) for group in groups] + [anywhere()],
        whole(1)[0],
        grid=(1,),
    )(place, *[out(group) for group in groups], order)


def project_kernel(
    place_ref, scalar_ref, own_ref, other_ref, reward_ref, weight_ref,
    guided_ref, grad_ref, keep_ref, send_ref,
):
    rows = own_ref.shape[1]
    half = guided_ref.shape[1]
    heads = own_ref.shape[0]
    blocks = heads // 2
    deep = 2 * HDIM
    first = place_ref[0] == 0
    gate, strength = scalar_ref[0], scalar_ref[1]
    total = None
    for block in range(blocks):
        head = 2 * block
        columns = jnp.concatenate(
            [
                jnp.concatenate([own_ref[head], own_ref[head + 1]], axis=1),
                jnp.concatenate([other_ref[head], other_ref[head + 1]], axis=1),
            ],
            axis=0,
        )
        part = jnp.dot(
            columns, weight_ref[block * deep : (block + 1) * deep], preferred_element_type=F32
        )
        total = part if total is None else total + part
    branch_out = (gate * total).astype(BF).astype(F32)
    own_out, other_out = branch_out[:rows], branch_out[rows:]
    cond = jnp.where(first, own_out, other_out)
    uncond = jnp.where(first, other_out, own_out)
    guided = uncond + strength * (cond - uncond)
    guided_ref[...] = guided.astype(BF)
    reward = jnp.where(first, reward_ref[:, :half], reward_ref[:, half:]).astype(F32)
    resid = reward - guided
    own_coeff = gate * jnp.where(first, strength, 1.0 - strength)
    other_coeff = gate * jnp.where(first, 1.0 - strength, strength)
    grad = jnp.concatenate([own_coeff * resid, other_coeff * resid], axis=0).astype(BF)
    grad_ref[...] = grad
    for block in range(blocks):
        part = lax.dot_general(
            grad, weight_ref[block * deep : (block + 1) * deep], NT, preferred_element_type=F32
        )
        for odd in range(2):
            lanes = part[:, lanes_of(odd)]
            keep_ref[2 * block + odd] = lanes[:rows]
            send_ref[2 * block + odd] = lanes[rows:].astype(BF)


def project(place, scalars, own, other, reward, weight):
    heads, rows, _ = own.shape
    half = reward.shape[1] // 2
    return call(
        project_kernel,
        "project",
        (
            spilled((rows, half)),
            kept((2 * rows, half)),
            kept((heads, rows, HDIM), F32),
            kept((heads, rows, HDIM)),
        ),
        [scalars_spec(), scalars_spec()] + whole(2) + [full(reward)] + whole(1),
        [pl.BlockSpec((rows, half), lambda i: (0, 0))] + whole(3),
        grid=(1,),
    )(place, scalars, pin(own), pin(other), out(reward), pin(weight))


def weight_kernel(place_ref, own_ref, other_ref, grad_ref, order_ref, *refs):
    grad = grad_ref[...]
    for dy, ref in enumerate(refs):
        for dx in range(4):
            head = head_of(place_ref, dx, dy)
            flipped = jnp.concatenate([own_ref[head].T, other_ref[head].T], axis=1)
            ref[dx] = jnp.dot(flipped, grad, preferred_element_type=F32).astype(BF)


def weight_gradient(place, own, other, grad, order):
    group = spilled((4, HDIM, grad.shape[1]))
    return call(
        weight_kernel,
        "weight_gradient",
        (group,) * 4,
        [scalars_spec()] + whole(3) + [anywhere()],
        [full(group)] * 4,
        grid=(1,),
    )(place, pin(own), pin(other), pin(grad), order)


def add_kernel(keep_ref, got_ref, out_ref):
    out_ref[...] = (keep_ref[...] + got_ref[...].astype(F32)).astype(BF)


def add_after(keep, got):
    return call(add_kernel, "add_after", kept(got.shape), whole(2))(pin(keep), pin(got))


def slices_kernel(place_ref, *refs):
    arrays, out_refs, held = refs[:4], refs[4:-1], refs[-1]
    deep = out_refs[0].shape[0]
    held[...] = sum(ref[...].astype(F32) for ref in arrays)
    for step, ref in enumerate(out_refs):
        start = pl.multiple_of(((place_ref[17] + step) & 7) * deep, deep)
        ref[...] = held[pl.ds(start, deep), :].astype(ref.dtype)


def z_slices(place, arrays):
    rows, wide = arrays[0].shape
    target = spilled((rows // 8, wide))
    return call(
        slices_kernel,
        "z_slices",
        (target,) * 8,
        [scalars_spec()] + [full(array) for array in arrays],
        [full(target)] * 8,
        grid=(1,),
        flops=10000000000,
        scratch_shapes=[pltpu.VMEM((rows, wide), F32)],
    )(place, *[out(array) for array in arrays])


def total_kernel(*refs):
    in_refs, out_ref = refs[:-2], refs[-1]
    total = in_refs[0][...].astype(F32)
    for ref in in_refs[1:]:
        total = total + ref[...].astype(F32)
    out_ref[...] = total


def total_of(arrays, order):
    return call(
        total_kernel,
        "total_of",
        kept(arrays[0].shape, F32),
        [full(array) for array in arrays] + [anywhere()],
        whole(1)[0],
        grid=(1,),
    )(*arrays, out(order))


def swap_cfg(value):
    return lax.ppermute(value, "cfg", [(0, 1), (1, 0)])


def shift_y(value, step):
    pairs = [(i, (i // 4) * 4 + (i % 4 + step) % 4) for i in range(8)]
    return lax.ppermute(value, "fsdp", pairs)


def shift_x(value, step):
    pairs = []
    for fsdp in range(8):
        for seq in range(16):
            x = ((fsdp // 4) * 2 + seq // 8 + step) % 4
            target = ((x // 2) * 4 + fsdp % 4) * 16 + (x % 2) * 8 + seq % 8
            pairs.append((fsdp * 16 + seq, target))
    return lax.ppermute(value, ("fsdp", "seq"), pairs)


def gather_groups(piece):
    right, left, far = shift_x(piece, -1), shift_x(piece, 1), shift_x(piece, 2)
    near = jnp.stack([piece, right])
    past = jnp.stack([far, left])
    near_left, near_right = shift_y(near, 1), shift_y(near, -1)
    past_left, past_right = shift_y(past, 1), shift_y(past, -1)
    near_far = shift_y(near_left, 1)
    past_far = shift_y(past_right, -1)
    return (near, near_right, near_far, near_left, past, past_right, past_far, past_left)


def group_kernel(*refs):
    in_refs, out_refs = refs[:4], refs[5:]
    for slot, target in enumerate(out_refs):
        total = sum(ref[slot].astype(F32) for ref in in_refs)
        target[...] = total.astype(target.dtype)


def group_sums(groups, order):
    shape = groups[0].shape[1:]
    outs = (spilled(shape, F32),) + (spilled(shape),) * 3
    return call(
        group_kernel,
        "group_sums",
        outs,
        [full(group) for group in groups] + [anywhere()],
        [full(target) for target in outs],
        grid=(1,),
        flops=10000000000,
    )(*[out(group) for group in groups], out(order))


def scatter_first(groups):
    return [groups[0]] + [shift_y(groups[step], step) for step in range(1, 4)]


def scatter_rest(place, groups, order, packed):
    sums = group_sums(groups, packed)
    ring = [sums[0]] + [shift_x(sums[step], step) for step in range(1, 4)]
    slices = z_slices(place, ring)
    parts = [slices[0]]
    for step in range(1, 8):
        pairs = [(i, (i & 8) + ((i + step) & 7)) for i in range(16)]
        parts.append(lax.ppermute(slices[step], "seq", pairs))
    return total_of(parts, order)


def over_seq(array):
    return lax.all_to_all(array, "seq", split_axis=0, concat_axis=0, tiled=True)


def over_z(array):
    groups = [list(range(8)), list(range(8, 16))]
    return lax.all_to_all(
        array, "seq", split_axis=0, concat_axis=0, axis_index_groups=groups, tiled=True
    )


def join_kernel(place_ref, own_ref, other_ref, order_ref, out_ref):
    first = place_ref[0] == 0
    half = own_ref.shape[1]
    out_ref[:, :half] = jnp.where(first, own_ref[...], other_ref[...])
    out_ref[:, half:] = jnp.where(first, other_ref[...], own_ref[...])


def joined(place, own, other, order, where=out):
    rows, half = own.shape
    return call(
        join_kernel,
        "joined",
        shaped((rows, 2 * half), own.dtype),
        [scalars_spec(), full(own), full(other), anywhere()],
        pl.BlockSpec((rows, 2 * half), lambda i: (0, 0)),
        grid=(1,),
    )(place, where(own), where(other), out(order))


def places():
    cfg = lax.axis_index("cfg")
    fsdp = lax.axis_index("fsdp")
    x = (fsdp >> 2) * 2 + (lax.axis_index("seq") >> 3)
    y = fsdp & 3
    slots = jnp.arange(16)
    there = (x + (slots & 3)) & 3
    block = (there >> 1) * 4 + ((y + (slots >> 2)) & 3)
    table = 2 * block + (there & 1)
    return jnp.concatenate([cfg[None], table, (lax.axis_index("seq") & 7)[None]]).astype(jnp.int32)


def local(query_act, key_act, value_act, out_weight, reward_dir, guide_index, step_index):
    place = places()
    moment = step_index[0].astype(F32)
    gate = jnp.cos(0.5 * jnp.pi * (moment + 0.5) / STEPS)
    strength = 1.0 + GUIDE_STEP * guide_index[0].astype(F32)
    scalars = jnp.stack([gate, strength])
    half = out_weight.shape[1] // 2
    own_half = jnp.where(place[0] == 0, out_weight[:, :half], out_weight[:, half:])
    piece = over_z(jnp.broadcast_to(own_half[None], (8,) + own_half.shape)).reshape(-1, half)
    groups = gather_groups(piece)
    qkv = over_seq(pack_heads(query_act[0, 0], key_act[0, 0], value_act[0, 0]))
    mixed_h, probs = attend_forward(qkv, *groups)
    mixed = over_seq(mixed_h)
    weight = assemble(place, groups, mixed)
    mixed_other = swap_cfg(mixed)
    guided, grad_out, keep, send = project(
        place, scalars, mixed, mixed_other, reward_dir[0], weight
    )
    grad_mixed = add_after(keep, swap_cfg(send))
    parts = weight_gradient(place, mixed, mixed_other, grad_out, grad_mixed)
    grad_h = over_seq(grad_mixed)
    parts = scatter_first(parts)
    packed = attend_backward(qkv, mixed_h, grad_h, probs, parts[0])
    guided_all = joined(place, guided, swap_cfg(guided), packed)
    last = over_seq(packed)
    grad_half = scatter_rest(place, parts, guided_all, packed)
    grad_query, grad_key, grad_value = unpack_heads(last, 3)
    grad_weight = joined(place, grad_half, swap_cfg(grad_half), grad_query, pin)
    return (
        guided_all[None],
        grad_query[None, None],
        grad_key[None, None],
        grad_value[None, None],
        grad_weight,
    )


def solution(mesh):
    placed = (
        P("cfg", "fsdp", "seq", None),
        P("cfg", "fsdp", "seq", None),
        P("cfg", "fsdp", "seq", None),
        P(("fsdp", "seq"), None),
        P("fsdp", "seq", None),
        P(),
        P(),
    )
    return jax.shard_map(
        local,
        mesh=mesh,
        in_specs=placed,
        out_specs=(
            P("fsdp", "seq", None),
            P("cfg", "fsdp", "seq", None),
            P("cfg", "fsdp", "seq", None),
            P("cfg", "fsdp", "seq", None),
            P(("fsdp", "seq"), None),
        ),
        check_vma=False,
    )
```

```python
import functools

import jax
import jax.numpy as jnp
from jax import lax
from jax.experimental import pallas as pl
from jax.experimental.pallas import tpu as pltpu
from jax.sharding import PartitionSpec as P

HDIM = 128
STEPS = 50
GUIDE_STEP = 0.04
LOG2E = 1.4426950408889634
BF = jnp.bfloat16
F32 = jnp.float32
NT = (((1,), (1,)), ((), ()))
VMEM_LIMIT = 20 * 1024 * 1024


def params():
    return pltpu.CompilerParams(vmem_limit_bytes=VMEM_LIMIT)


def whole(count):
    return [pl.BlockSpec(memory_space=pltpu.VMEM) for _ in range(count)]


def anywhere():
    return pl.BlockSpec(memory_space=pl.ANY)


def full(array):
    rank = len(array.shape)
    return pl.BlockSpec(array.shape, lambda i: (0,) * rank)


def scalars_spec():
    return pl.BlockSpec(memory_space=pltpu.SMEM)


def call(kernel, name, out_shape, in_specs, out_specs=None, flops=1, **kwargs):
    if out_specs is None:
        out_specs = whole(len(out_shape)) if isinstance(out_shape, tuple) else whole(1)[0]
    return pl.pallas_call(
        kernel,
        out_shape=out_shape,
        in_specs=in_specs,
        out_specs=tuple(out_specs) if isinstance(out_shape, tuple) else out_specs,
        compiler_params=params(),
        cost_estimate=pl.CostEstimate(flops=flops, bytes_accessed=1, transcendentals=0),
        name=name,
        **kwargs,
    )


def shaped(shape, dtype=BF):
    return jax.ShapeDtypeStruct(shape, dtype)


def kept(shape, dtype=BF):
    return pltpu.VMEM(shape, dtype)


def pin(array):
    return pltpu.with_memory_space_constraint(array, pltpu.VMEM)


def spilled(shape, dtype=BF):
    return pltpu.HBM(shape, dtype)


def out(array):
    return pltpu.with_memory_space_constraint(array, pltpu.HBM)


def ordered(orders):
    return [anywhere()] * len(orders)


def lanes_of(head):
    return slice(head * HDIM, (head + 1) * HDIM)


def pack_kernel(*refs):
    in_refs, out_ref = refs[:-1], refs[-1]
    rows = in_refs[0].shape[0]
    for head in range(out_ref.shape[0]):
        for place, ref in enumerate(in_refs):
            out_ref[head, place * rows : (place + 1) * rows, :] = ref[:, lanes_of(head)]


def pack_heads(*arrays):
    rows, width = arrays[0].shape
    return call(
        pack_kernel,
        "pack_heads",
        kept((width // HDIM, len(arrays) * rows, HDIM)),
        [full(array) for array in arrays],
        grid=(1,),
    )(*[out(array) for array in arrays])


def unpack_kernel(in_ref, *out_refs):
    rows = out_refs[0].shape[0]
    for head in range(in_ref.shape[0]):
        for place, ref in enumerate(out_refs):
            ref[:, lanes_of(head)] = in_ref[head, place * rows : (place + 1) * rows, :]


def unpack_heads(packed, count):
    target = shaped((packed.shape[1] // count, packed.shape[0] * HDIM))
    return call(
        unpack_kernel,
        "unpack_heads",
        (target,) * count,
        [full(packed)],
        [full(target)] * count,
        grid=(1,),
    )(packed)


CHUNK = 512


def forward_kernel(qkv_ref, *refs):
    out_ref, probs_ref, held, sems = refs[-4:]
    shards, total_rows, _ = qkv_ref.shape
    rows = total_rows // 3
    length = shards * rows
    keys = qkv_ref[:, rows : 2 * rows, :].reshape(length, HDIM)
    value_t = qkv_ref[:, 2 * rows :, :].reshape(length, HDIM).astype(F32).T.astype(BF)
    scale = HDIM ** (-0.5) * LOG2E
    take = CHUNK // rows
    copies = []
    for part in range(length // CHUNK):
        here = slice(part * take, (part + 1) * take)
        query = qkv_ref[here, :rows, :].reshape(CHUNK, HDIM)
        scores = lax.dot_general(keys, query, NT, preferred_element_type=F32)
        peak = jnp.max(scores, axis=0, keepdims=True) * scale
        weights = jnp.exp2(scores * scale - peak)
        total = jnp.sum(weights, axis=0, keepdims=True)
        probs = (weights * (1.0 / total)).astype(BF)
        lanes = pl.ds(part * CHUNK, CHUNK)
        held[:, lanes] = probs
        copy = pltpu.make_async_copy(held.at[:, lanes], probs_ref.at[:, lanes], sems.at[part])
        copy.start()
        copies.append(copy)
        mixed_t = jnp.dot(value_t, probs, preferred_element_type=F32)
        out_ref[here] = mixed_t.T.astype(BF).reshape(take, rows, HDIM)
    for copy in copies:
        copy.wait()


def attend_forward(qkv, *orders):
    shards, total_rows, _ = qkv.shape
    rows = total_rows // 3
    length = shards * rows
    return call(
        forward_kernel,
        "attend_forward",
        (kept((shards, rows, HDIM)), spilled((length, length))),
        whole(1) + ordered(orders),
        whole(1) + [anywhere()],
        scratch_shapes=[
            pltpu.VMEM((length, length), BF),
            pltpu.SemaphoreType.DMA((length // CHUNK,)),
        ],
    )(qkv, *[order if order.ndim == 1 else out(order) for order in orders])


def backward_kernel(qkv_ref, mixed_ref, grad_ref, probs_ref, *refs):
    out_ref, query_t, held, sems = refs[-4:]
    copies = []
    for part in range(sems.shape[0]):
        span = pl.ds(part * CHUNK, CHUNK)
        copies.append(pltpu.make_async_copy(probs_ref.at[span], held.at[span], sems.at[part]))
    for copy in copies:
        copy.start()
    shards, rows, _ = mixed_ref.shape
    length = shards * rows
    factor = HDIM ** (-0.5)
    grad = grad_ref[...].reshape(length, HDIM)
    mixed = mixed_ref[...].reshape(length, HDIM)
    product = grad.astype(F32) * mixed.astype(F32)
    inner = jnp.sum(product.T, axis=0, keepdims=True)
    query = qkv_ref[:, :rows, :].reshape(length, HDIM)
    chunk = CHUNK // 2
    take = chunk // rows
    for part in range(length // chunk):
        if part % 2 == 0:
            copies[part // 2].wait()
        here = slice(part * take, (part + 1) * take)
        probs = held[part * chunk : (part + 1) * chunk, :]
        keys = qkv_ref[here, rows : 2 * rows, :].reshape(chunk, HDIM)
        value = qkv_ref[here, 2 * rows :, :].reshape(chunk, HDIM)
        grad_value = jnp.dot(probs, grad, preferred_element_type=F32)
        out_ref[here, 2 * rows :, :] = grad_value.astype(BF).reshape(take, rows, HDIM)
        grad_probs = lax.dot_general(value, grad, NT, preferred_element_type=F32)
        grad_scores = (probs.astype(F32) * (grad_probs - inner)).astype(BF)
        grad_key = jnp.dot(grad_scores, query, preferred_element_type=F32) * factor
        out_ref[here, rows : 2 * rows, :] = grad_key.astype(BF).reshape(take, rows, HDIM)
        keys_t = keys.astype(F32).T.astype(BF)
        piece = jnp.dot(keys_t, grad_scores, preferred_element_type=F32)
        if part == 0:
            query_t[...] = piece
        else:
            query_t[...] += piece
    grad_query = (query_t[...] * factor).T.astype(BF)
    out_ref[:, :rows, :] = grad_query.reshape(shards, rows, HDIM)


def attend_backward(qkv, mixed, grad, probs, *orders):
    length = probs.shape[0]
    return call(
        backward_kernel,
        "attend_backward",
        kept(qkv.shape),
        [full(qkv), full(mixed), full(grad), anywhere()] + ordered(orders),
        whole(1)[0],
        grid=(1,),
        flops=16 * length * length * HDIM,
        scratch_shapes=[
            pltpu.VMEM((HDIM, length), F32),
            pltpu.VMEM((length, length), BF),
            pltpu.SemaphoreType.DMA((length // CHUNK,)),
        ],
    )(out(qkv), out(mixed), grad, out(probs), *[out(order) for order in orders])


def head_of(place_ref, dx, dy):
    return place_ref[1 + 4 * dy + dx]


def head_of(place_ref, dx, dy):
    return place_ref[1 + 4 * dy + dx]


def assemble_kernel(place_ref, *refs):
    groups, out_ref = refs[:-2], refs[-1]
    deep = groups[0].shape[1]
    for dy, (one, two) in enumerate(zip(groups[:4], groups[4:])):
        for dx in range(4):
            start = pl.multiple_of(head_of(place_ref, dx, dy) * deep, deep)
            out_ref[pl.ds(start, deep), :] = (one if dx < 2 else two)[dx % 2]


def assemble(place, groups, order):
    _, deep, wide = groups[0].shape
    return call(
        assemble_kernel,
        "assemble",
        kept((16 * deep, wide)),
        [scalars_spec()] + [full(group) for group in groups] + [anywhere()],
        whole(1)[0],
        grid=(1,),
        flops=10000000000,
    )(place, *[out(group) for group in groups], order)


def project_kernel(
    place_ref, scalar_ref, own_ref, other_ref, reward_ref, weight_ref,
    guided_ref, grad_ref, keep_ref, send_ref,
):
    rows = own_ref.shape[1]
    half = guided_ref.shape[1]
    heads = own_ref.shape[0]
    blocks = heads // 2
    deep = 2 * HDIM
    first = place_ref[0] == 0
    gate, strength = scalar_ref[0], scalar_ref[1]
    total = None
    for block in range(blocks):
        head = 2 * block
        columns = jnp.concatenate(
            [
                jnp.concatenate([own_ref[head], own_ref[head + 1]], axis=1),
                jnp.concatenate([other_ref[head], other_ref[head + 1]], axis=1),
            ],
            axis=0,
        )
        part = jnp.dot(
            columns, weight_ref[block * deep : (block + 1) * deep], preferred_element_type=F32
        )
        total = part if total is None else total + part
    branch_out = (gate * total).astype(BF).astype(F32)
    own_out, other_out = branch_out[:rows], branch_out[rows:]
    cond = jnp.where(first, own_out, other_out)
    uncond = jnp.where(first, other_out, own_out)
    guided = uncond + strength * (cond - uncond)
    guided_ref[...] = guided.astype(BF)
    reward = jnp.where(first, reward_ref[:, :half], reward_ref[:, half:]).astype(F32)
    resid = reward - guided
    own_coeff = gate * jnp.where(first, strength, 1.0 - strength)
    other_coeff = gate * jnp.where(first, 1.0 - strength, strength)
    grad = jnp.concatenate([own_coeff * resid, other_coeff * resid], axis=0).astype(BF)
    grad_ref[...] = grad
    for block in range(blocks):
        part = lax.dot_general(
            grad, weight_ref[block * deep : (block + 1) * deep], NT, preferred_element_type=F32
        )
        for odd in range(2):
            lanes = part[:, lanes_of(odd)]
            keep_ref[2 * block + odd] = lanes[:rows]
            send_ref[2 * block + odd] = lanes[rows:].astype(BF)


def project(place, scalars, own, other, reward, weight):
    heads, rows, _ = own.shape
    half = reward.shape[1] // 2
    return call(
        project_kernel,
        "project",
        (
            spilled((rows, half)),
            kept((2 * rows, half)),
            kept((heads, rows, HDIM), F32),
            kept((heads, rows, HDIM)),
        ),
        [scalars_spec(), scalars_spec()] + whole(2) + [full(reward)] + whole(1),
        [pl.BlockSpec((rows, half), lambda i: (0, 0))] + whole(3),
        grid=(1,),
    )(place, scalars, pin(own), pin(other), out(reward), pin(weight))


def weight_kernel(place_ref, own_ref, other_ref, grad_ref, order_ref, *refs):
    by_y, by_x = refs[:4], refs[4:]
    wide = by_x[0].shape[2]
    grad = grad_ref[...]
    for dx in range(4):
        for dy in range(4):
            head = head_of(place_ref, dx, dy)
            flipped = jnp.concatenate([own_ref[head].T, other_ref[head].T], axis=1)
            part = jnp.dot(flipped, grad, preferred_element_type=F32).astype(BF)
            by_y[dy][dx] = part[:, :wide]
            by_x[dx][dy] = part[:, wide:]


def weight_gradient(place, own, other, grad, order):
    group = spilled((4, HDIM, grad.shape[1] // 2))
    return call(
        weight_kernel,
        "weight_gradient",
        (group,) * 8,
        [scalars_spec()] + whole(3) + [anywhere()],
        [full(group)] * 8,
        grid=(1,),
    )(place, pin(own), pin(other), pin(grad), order)


def add_kernel(keep_ref, got_ref, out_ref):
    out_ref[...] = (keep_ref[...] + got_ref[...].astype(F32)).astype(BF)


def add_after(keep, got):
    return call(add_kernel, "add_after", kept(got.shape), whole(2))(pin(keep), pin(got))


def slices_kernel(place_ref, *refs):
    first, second, out_refs, held = refs[:4], refs[4:8], refs[8:-1], refs[-1]
    deep = out_refs[0].shape[0]
    wide = first[0].shape[1]
    held[:, :wide] = sum(ref[...].astype(F32) for ref in first)
    held[:, wide:] = sum(ref[...].astype(F32) for ref in second)
    for step, ref in enumerate(out_refs):
        start = pl.multiple_of(((place_ref[17] + step) & 7) * deep, deep)
        ref[...] = held[pl.ds(start, deep), :].astype(ref.dtype)


def z_slices(place, arrays):
    rows, wide = arrays[0].shape
    target = spilled((rows // 8, 2 * wide))
    return call(
        slices_kernel,
        "z_slices",
        (target,) * 8,
        [scalars_spec()] + [full(array) for array in arrays],
        [full(target)] * 8,
        grid=(1,),
        flops=15000000000,
        scratch_shapes=[pltpu.VMEM((rows, 2 * wide), F32)],
    )(place, *[out(array) for array in arrays])


def total_kernel(*refs):
    in_refs, out_ref = refs[:-2], refs[-1]
    total = in_refs[0][...].astype(F32)
    for ref in in_refs[1:]:
        total = total + ref[...].astype(F32)
    out_ref[...] = total


def total_of(arrays, order):
    return call(
        total_kernel,
        "total_of",
        kept(arrays[0].shape, F32),
        [full(array) for array in arrays] + [anywhere()],
        whole(1)[0],
        grid=(1,),
    )(*arrays, out(order))


def swap_cfg(value):
    return lax.ppermute(value, "cfg", [(0, 1), (1, 0)])


def shift_y(value, step):
    pairs = [(i, (i // 4) * 4 + (i % 4 + step) % 4) for i in range(8)]
    return lax.ppermute(value, "fsdp", pairs)


def shift_x(value, step):
    pairs = []
    for fsdp in range(8):
        for seq in range(16):
            x = ((fsdp // 4) * 2 + seq // 8 + step) % 4
            target = ((x // 2) * 4 + fsdp % 4) * 16 + (x % 2) * 8 + seq % 8
            pairs.append((fsdp * 16 + seq, target))
    return lax.ppermute(value, ("fsdp", "seq"), pairs)


def gather_groups(piece):
    right, left, far = shift_x(piece, -1), shift_x(piece, 1), shift_x(piece, 2)
    near = jnp.stack([piece, right])
    past = jnp.stack([far, left])
    near_left, near_right = shift_y(near, 1), shift_y(near, -1)
    past_left, past_right = shift_y(past, 1), shift_y(past, -1)
    near_far = shift_y(near_left, 1)
    past_far = shift_y(past_right, -1)
    return (near, near_right, near_far, near_left, past, past_right, past_far, past_left)


def group_kernel(*refs):
    in_refs, out_refs = refs[:8], refs[9:]
    for side in range(2):
        for slot in range(4):
            total = sum(ref[slot].astype(F32) for ref in in_refs[4 * side : 4 * side + 4])
            target = out_refs[4 * side + slot]
            target[...] = total.astype(target.dtype)


def group_sums(groups, order):
    shape = groups[0].shape[1:]
    outs = ((spilled(shape, F32),) + (spilled(shape),) * 3) * 2
    return call(
        group_kernel,
        "group_sums",
        outs,
        [full(group) for group in groups] + [anywhere()],
        [full(target) for target in outs],
        grid=(1,),
        flops=15000000000,
    )(*[out(group) for group in groups], out(order))


def scatter_first(groups):
    by_y, by_x = groups[:4], groups[4:]
    first = [by_y[0]] + [shift_y(by_y[step], step) for step in range(1, 4)]
    second = [by_x[0]] + [shift_x(by_x[step], step) for step in range(1, 4)]
    return first + second


def scatter_rest(place, groups, order, packed):
    sums = group_sums(groups, packed)
    first = [sums[0]] + [shift_x(sums[step], step) for step in range(1, 4)]
    second = [sums[4]] + [shift_y(sums[4 + step], step) for step in range(1, 4)]
    slices = z_slices(place, first + second)
    parts = [slices[0]]
    for step in range(1, 8):
        pairs = [(i, (i & 8) + ((i + step) & 7)) for i in range(16)]
        parts.append(lax.ppermute(slices[step], "seq", pairs))
    return total_of(parts, order)


def over_seq(array):
    return lax.all_to_all(array, "seq", split_axis=0, concat_axis=0, tiled=True)


def over_z(array):
    groups = [list(range(8)), list(range(8, 16))]
    return lax.all_to_all(
        array, "seq", split_axis=0, concat_axis=0, axis_index_groups=groups, tiled=True
    )


def join_kernel(place_ref, own_ref, other_ref, order_ref, out_ref):
    first = place_ref[0] == 0
    half = own_ref.shape[1]
    out_ref[:, :half] = jnp.where(first, own_ref[...], other_ref[...])
    out_ref[:, half:] = jnp.where(first, other_ref[...], own_ref[...])


def joined(place, own, other, order, where=out):
    rows, half = own.shape
    return call(
        join_kernel,
        "joined",
        shaped((rows, 2 * half), own.dtype),
        [scalars_spec(), full(own), full(other), anywhere()],
        pl.BlockSpec((rows, 2 * half), lambda i: (0, 0)),
        grid=(1,),
    )(place, where(own), where(other), out(order))


def places():
    cfg = lax.axis_index("cfg")
    fsdp = lax.axis_index("fsdp")
    x = (fsdp >> 2) * 2 + (lax.axis_index("seq") >> 3)
    y = fsdp & 3
    slots = jnp.arange(16)
    there = (x + (slots & 3)) & 3
    block = (there >> 1) * 4 + ((y + (slots >> 2)) & 3)
    table = 2 * block + (there & 1)
    return jnp.concatenate([cfg[None], table, (lax.axis_index("seq") & 7)[None]]).astype(jnp.int32)


def local(query_act, key_act, value_act, out_weight, reward_dir, guide_index, step_index):
    place = places()
    moment = step_index[0].astype(F32)
    gate = jnp.cos(0.5 * jnp.pi * (moment + 0.5) / STEPS)
    strength = 1.0 + GUIDE_STEP * guide_index[0].astype(F32)
    scalars = jnp.stack([gate, strength])
    half = out_weight.shape[1] // 2
    own_half = jnp.where(place[0] == 0, out_weight[:, :half], out_weight[:, half:])
    piece = over_z(jnp.broadcast_to(own_half[None], (8,) + own_half.shape)).reshape(-1, half)
    groups = gather_groups(piece)
    qkv = over_seq(pack_heads(query_act[0, 0], key_act[0, 0], value_act[0, 0]))
    mixed_h, probs = attend_forward(qkv, groups[1], groups[3], groups[5], groups[7], place, scalars)
    mixed = over_seq(mixed_h)
    weight = assemble(place, groups, mixed)
    mixed_other = swap_cfg(mixed)
    guided, grad_out, keep, send = project(
        place, scalars, mixed, mixed_other, reward_dir[0], weight
    )
    grad_mixed = add_after(keep, swap_cfg(send))
    parts = weight_gradient(place, mixed, mixed_other, grad_out, grad_mixed)
    grad_h = over_seq(grad_mixed)
    parts = scatter_first(parts)
    packed = attend_backward(qkv, mixed_h, grad_h, probs, parts[0])
    guided_all = joined(place, guided, swap_cfg(guided), packed)
    last = over_seq(packed)
    grad_half = scatter_rest(place, parts, guided_all, packed)
    grad_query, grad_key, grad_value = unpack_heads(last, 3)
    grad_weight = joined(place, grad_half, swap_cfg(grad_half), grad_query, pin)
    return (
        guided_all[None],
        grad_query[None, None],
        grad_key[None, None],
        grad_value[None, None],
        grad_weight,
    )


def solution(mesh):
    placed = (
        P("cfg", "fsdp", "seq", None),
        P("cfg", "fsdp", "seq", None),
        P("cfg", "fsdp", "seq", None),
        P(("fsdp", "seq"), None),
        P("fsdp", "seq", None),
        P(),
        P(),
    )
    return jax.shard_map(
        local,
        mesh=mesh,
        in_specs=placed,
        out_specs=(
            P("fsdp", "seq", None),
            P("cfg", "fsdp", "seq", None),
            P("cfg", "fsdp", "seq", None),
            P("cfg", "fsdp", "seq", None),
            P(("fsdp", "seq"), None),
        ),
        check_vma=False,
    )
```

```python
import functools

import jax
import jax.numpy as jnp
from jax import lax
from jax.experimental import pallas as pl
from jax.experimental.pallas import tpu as pltpu
from jax.sharding import PartitionSpec as P

HDIM = 128
STEPS = 50
GUIDE_STEP = 0.04
LOG2E = 1.4426950408889634
BF = jnp.bfloat16
F32 = jnp.float32
NT = (((1,), (1,)), ((), ()))
VMEM_LIMIT = 20 * 1024 * 1024


def params():
    return pltpu.CompilerParams(vmem_limit_bytes=VMEM_LIMIT)


def whole(count):
    return [pl.BlockSpec(memory_space=pltpu.VMEM) for _ in range(count)]


def anywhere():
    return pl.BlockSpec(memory_space=pl.ANY)


def full(array):
    rank = len(array.shape)
    return pl.BlockSpec(array.shape, lambda i: (0,) * rank)


def scalars_spec():
    return pl.BlockSpec(memory_space=pltpu.SMEM)


def call(kernel, name, out_shape, in_specs, out_specs=None, flops=1, **kwargs):
    if out_specs is None:
        out_specs = whole(len(out_shape)) if isinstance(out_shape, tuple) else whole(1)[0]
    return pl.pallas_call(
        kernel,
        out_shape=out_shape,
        in_specs=in_specs,
        out_specs=tuple(out_specs) if isinstance(out_shape, tuple) else out_specs,
        compiler_params=params(),
        cost_estimate=pl.CostEstimate(flops=flops, bytes_accessed=1, transcendentals=0),
        name=name,
        **kwargs,
    )


def shaped(shape, dtype=BF):
    return jax.ShapeDtypeStruct(shape, dtype)


def kept(shape, dtype=BF):
    return pltpu.VMEM(shape, dtype)


def pin(array):
    return pltpu.with_memory_space_constraint(array, pltpu.VMEM)


def spilled(shape, dtype=BF):
    return pltpu.HBM(shape, dtype)


def out(array):
    return pltpu.with_memory_space_constraint(array, pltpu.HBM)


def ordered(orders):
    return [anywhere()] * len(orders)


def lanes_of(head):
    return slice(head * HDIM, (head + 1) * HDIM)


def pack_kernel(*refs):
    in_refs, out_ref = refs[:-1], refs[-1]
    rows = in_refs[0].shape[0]
    for head in range(out_ref.shape[0]):
        for place, ref in enumerate(in_refs):
            out_ref[head, place * rows : (place + 1) * rows, :] = ref[:, lanes_of(head)]


def pack_heads(*arrays):
    rows, width = arrays[0].shape
    return call(
        pack_kernel,
        "pack_heads",
        kept((width // HDIM, len(arrays) * rows, HDIM)),
        [full(array) for array in arrays],
        grid=(1,),
    )(*[out(array) for array in arrays])


def unpack_kernel(in_ref, *out_refs):
    rows = out_refs[0].shape[0]
    for head in range(in_ref.shape[0]):
        for place, ref in enumerate(out_refs):
            ref[:, lanes_of(head)] = in_ref[head, place * rows : (place + 1) * rows, :]


def unpack_heads(packed, count):
    target = shaped((packed.shape[1] // count, packed.shape[0] * HDIM))
    return call(
        unpack_kernel,
        "unpack_heads",
        (target,) * count,
        [full(packed)],
        [full(target)] * count,
        grid=(1,),
    )(packed)


CHUNK = 512


def forward_kernel(qkv_ref, *refs):
    out_ref, probs_ref, held, sems = refs[-4:]
    shards, total_rows, _ = qkv_ref.shape
    rows = total_rows // 3
    length = shards * rows
    keys = qkv_ref[:, rows : 2 * rows, :].reshape(length, HDIM)
    value_t = qkv_ref[:, 2 * rows :, :].reshape(length, HDIM).astype(F32).T.astype(BF)
    scale = HDIM ** (-0.5) * LOG2E
    take = CHUNK // rows
    copies = []
    for part in range(length // CHUNK):
        here = slice(part * take, (part + 1) * take)
        query = qkv_ref[here, :rows, :].reshape(CHUNK, HDIM)
        scores = lax.dot_general(keys, query, NT, preferred_element_type=F32)
        peak = jnp.max(scores, axis=0, keepdims=True) * scale
        weights = jnp.exp2(scores * scale - peak)
        total = jnp.sum(weights, axis=0, keepdims=True)
        probs = (weights * (1.0 / total)).astype(BF)
        lanes = pl.ds(part * CHUNK, CHUNK)
        held[:, lanes] = probs
        copy = pltpu.make_async_copy(held.at[:, lanes], probs_ref.at[:, lanes], sems.at[part])
        copy.start()
        copies.append(copy)
        mixed_t = jnp.dot(value_t, probs, preferred_element_type=F32)
        out_ref[here] = mixed_t.T.astype(BF).reshape(take, rows, HDIM)
    for copy in copies:
        copy.wait()


def attend_forward(qkv, *orders):
    shards, total_rows, _ = qkv.shape
    rows = total_rows // 3
    length = shards * rows
    return call(
        forward_kernel,
        "attend_forward",
        (kept((shards, rows, HDIM)), spilled((length, length))),
        whole(1) + ordered(orders),
        whole(1) + [anywhere()],
        scratch_shapes=[
            pltpu.VMEM((length, length), BF),
            pltpu.SemaphoreType.DMA((length // CHUNK,)),
        ],
    )(qkv, *[order if order.ndim == 1 else out(order) for order in orders])


def backward_kernel(qkv_ref, mixed_ref, grad_ref, probs_ref, *refs):
    out_ref, query_t, inner, held, sems = refs[-5:]
    shards, rows, _ = mixed_ref.shape
    length = shards * rows
    factor = HDIM ** (-0.5)
    chunk = CHUNK // 2
    take = chunk // rows

    def fetch(part):
        span = pl.ds(pl.multiple_of(part * CHUNK, CHUNK), CHUNK)
        return pltpu.make_async_copy(probs_ref.at[span], held.at[span], sems.at[part])

    for part in range(length // CHUNK):
        fetch(part).start()
    product = grad_ref[...].astype(F32) * mixed_ref[...].astype(F32)
    inner[...] = jnp.sum(product.reshape(length, HDIM).T, axis=0, keepdims=True)
    query_t[...] = jnp.zeros_like(query_t)

    def one_chunk(part):
        here = pl.ds(part * take, take)
        grad = grad_ref[...].reshape(length, HDIM)
        query = qkv_ref[:, :rows, :].reshape(length, HDIM)
        probs = held[pl.ds(pl.multiple_of(part * chunk, chunk), chunk), :]
        keys = qkv_ref[here, rows : 2 * rows, :].reshape(chunk, HDIM)
        value = qkv_ref[here, 2 * rows :, :].reshape(chunk, HDIM)
        grad_value = jnp.dot(probs, grad, preferred_element_type=F32)
        out_ref[here, 2 * rows :, :] = grad_value.astype(BF).reshape(take, rows, HDIM)
        grad_probs = lax.dot_general(value, grad, NT, preferred_element_type=F32)
        grad_scores = (probs.astype(F32) * (grad_probs - inner[...])).astype(BF)
        grad_key = jnp.dot(grad_scores, query, preferred_element_type=F32) * factor
        out_ref[here, rows : 2 * rows, :] = grad_key.astype(BF).reshape(take, rows, HDIM)
        query_t[...] += jnp.dot(keys.T, grad_scores, preferred_element_type=F32)

    @pl.loop(0, length // CHUNK)
    def _(part):
        fetch(part).wait()
        one_chunk(2 * part)
        one_chunk(2 * part + 1)

    grad_query = (query_t[...] * factor).T.astype(BF)
    out_ref[:, :rows, :] = grad_query.reshape(shards, rows, HDIM)


def attend_backward(qkv, mixed, grad, probs, *orders):
    length = probs.shape[0]
    return call(
        backward_kernel,
        "attend_backward",
        kept(qkv.shape),
        [full(qkv), full(mixed), full(grad), anywhere()] + ordered(orders),
        whole(1)[0],
        grid=(1,),
        flops=16 * length * length * HDIM,
        scratch_shapes=[
            pltpu.VMEM((HDIM, length), F32),
            pltpu.VMEM((1, length), F32),
            pltpu.VMEM((length, length), BF),
            pltpu.SemaphoreType.DMA((length // CHUNK,)),
        ],
    )(out(qkv), out(mixed), grad, out(probs), *[out(order) for order in orders])


def head_of(place_ref, dx, dy):
    return place_ref[1 + 4 * dy + dx]


def head_of(place_ref, dx, dy):
    return place_ref[1 + 4 * dy + dx]


def assemble_kernel(place_ref, *refs):
    groups, out_ref = refs[:-2], refs[-1]
    deep = groups[0].shape[1]
    for dy, (one, two) in enumerate(zip(groups[:4], groups[4:])):
        for dx in range(4):
            start = pl.multiple_of(head_of(place_ref, dx, dy) * deep, deep)
            out_ref[pl.ds(start, deep), :] = (one if dx < 2 else two)[dx % 2]


def assemble(place, groups, order):
    _, deep, wide = groups[0].shape
    return call(
        assemble_kernel,
        "assemble",
        kept((16 * deep, wide)),
        [scalars_spec()] + [full(group) for group in groups] + [anywhere()],
        whole(1)[0],
        grid=(1,),
        flops=10000000000,
    )(place, *[group if i % 4 == 2 else out(group) for i, group in enumerate(groups)], order)


def project_kernel(
    place_ref, scalar_ref, own_ref, other_ref, reward_ref, weight_ref,
    guided_ref, grad_ref, keep_ref, send_ref,
):
    rows = own_ref.shape[1]
    half = guided_ref.shape[1]
    heads = own_ref.shape[0]
    blocks = heads // 2
    deep = 2 * HDIM
    first = place_ref[0] == 0
    gate, strength = scalar_ref[0], scalar_ref[1]
    total = None
    for block in range(blocks):
        head = 2 * block
        columns = jnp.concatenate(
            [
                jnp.concatenate([own_ref[head], own_ref[head + 1]], axis=1),
                jnp.concatenate([other_ref[head], other_ref[head + 1]], axis=1),
            ],
            axis=0,
        )
        part = jnp.dot(
            columns, weight_ref[block * deep : (block + 1) * deep], preferred_element_type=F32
        )
        total = part if total is None else total + part
    branch_out = (gate * total).astype(BF).astype(F32)
    own_out, other_out = branch_out[:rows], branch_out[rows:]
    cond = jnp.where(first, own_out, other_out)
    uncond = jnp.where(first, other_out, own_out)
    guided = uncond + strength * (cond - uncond)
    guided_ref[...] = guided.astype(BF)
    reward = jnp.where(first, reward_ref[:, :half], reward_ref[:, half:]).astype(F32)
    resid = reward - guided
    own_coeff = gate * jnp.where(first, strength, 1.0 - strength)
    other_coeff = gate * jnp.where(first, 1.0 - strength, strength)
    grad = jnp.concatenate([own_coeff * resid, other_coeff * resid], axis=0).astype(BF)
    grad_ref[...] = grad
    for block in range(blocks):
        part = lax.dot_general(
            grad, weight_ref[block * deep : (block + 1) * deep], NT, preferred_element_type=F32
        )
        for odd in range(2):
            lanes = part[:, lanes_of(odd)]
            keep_ref[2 * block + odd] = lanes[:rows]
            send_ref[2 * block + odd] = lanes[rows:].astype(BF)


def project(place, scalars, own, other, reward, weight):
    heads, rows, _ = own.shape
    half = reward.shape[1] // 2
    return call(
        project_kernel,
        "project",
        (
            spilled((rows, half)),
            kept((2 * rows, half)),
            kept((heads, rows, HDIM), F32),
            kept((heads, rows, HDIM)),
        ),
        [scalars_spec(), scalars_spec()] + whole(2) + [full(reward)] + whole(1),
        [pl.BlockSpec((rows, half), lambda i: (0, 0))] + whole(3),
        grid=(1,),
    )(place, scalars, pin(own), pin(other), out(reward), pin(weight))


def weight_kernel(place_ref, own_ref, other_ref, grad_ref, order_ref, *refs):
    grad = grad_ref[...]
    for dy, ref in enumerate(refs):
        for dx in range(4):
            head = head_of(place_ref, dx, dy)
            flipped = jnp.concatenate([own_ref[head].T, other_ref[head].T], axis=1)
            ref[dx] = jnp.dot(flipped, grad, preferred_element_type=F32).astype(BF)


def weight_gradient(place, own, other, grad, order):
    group = spilled((4, HDIM, grad.shape[1]))
    return call(
        weight_kernel,
        "weight_gradient",
        (group,) * 4,
        [scalars_spec()] + whole(3) + [anywhere()],
        [full(group)] * 4,
        grid=(1,),
    )(place, pin(own), pin(other), pin(grad), order)


def add_kernel(keep_ref, got_ref, out_ref):
    out_ref[...] = (keep_ref[...] + got_ref[...].astype(F32)).astype(BF)


def add_after(keep, got):
    return call(add_kernel, "add_after", kept(got.shape), whole(2))(pin(keep), pin(got))


def halves_kernel(place_ref, *refs):
    arrays, keep_ref, send_ref, held = refs[:4], refs[-3], refs[-2], refs[-1]
    rows = keep_ref.shape[0]
    held[...] = sum(ref[...].astype(F32) for ref in arrays)
    start = pl.multiple_of((place_ref[17] >> 2) * rows, rows)
    other = pl.multiple_of(rows - start, rows)
    keep_ref[...] = held[pl.ds(start, rows), :]
    send_ref[...] = held[pl.ds(other, rows), :].astype(BF)


def z_halves(place, arrays, order):
    rows, wide = arrays[0].shape
    outs = (spilled((rows // 2, wide), F32), spilled((rows // 2, wide)))
    return call(
        halves_kernel,
        "z_halves",
        outs,
        [scalars_spec()] + [full(array) for array in arrays] + [anywhere()],
        [full(target) for target in outs],
        grid=(1,),
        flops=10000000000,
        scratch_shapes=[pltpu.VMEM((rows, wide), F32)],
    )(place, *[out(array) for array in arrays], out(order))


def quarters_kernel(place_ref, keep_ref, got_ref, *refs):
    out_refs, held = refs[:-1], refs[-1]
    deep = out_refs[0].shape[0]
    held[...] = keep_ref[...] + got_ref[...].astype(F32)
    for step, ref in enumerate(out_refs):
        start = pl.multiple_of(((place_ref[17] + step) & 3) * deep, deep)
        ref[...] = held[pl.ds(start, deep), :].astype(ref.dtype)


def z_quarters(place, keep, got):
    rows, wide = keep.shape
    target = (rows // 4, wide)
    return call(
        quarters_kernel,
        "z_quarters",
        (kept(target, F32),) + (kept(target),) * 3,
        [scalars_spec(), full(keep), full(got)],
        whole(4),
        grid=(1,),
        scratch_shapes=[pltpu.VMEM((rows, wide), F32)],
    )(place, keep, got)


def total_kernel(*refs):
    in_refs, out_ref = refs[:-1], refs[-1]
    out_ref[...] = sum(ref[...].astype(F32) for ref in in_refs)


def total_of(arrays):
    return call(
        total_kernel,
        "total_of",
        kept(arrays[0].shape, F32),
        whole(len(arrays)),
        whole(1)[0],
    )(*[pin(array) for array in arrays])


def swap_cfg(value):
    return lax.ppermute(value, "cfg", [(0, 1), (1, 0)])


def shift_y(value, step):
    pairs = [(i, (i // 4) * 4 + (i % 4 + step) % 4) for i in range(8)]
    return lax.ppermute(value, "fsdp", pairs)


def shift_x(value, step):
    pairs = []
    for fsdp in range(8):
        for seq in range(16):
            x = ((fsdp // 4) * 2 + seq // 8 + step) % 4
            target = ((x // 2) * 4 + fsdp % 4) * 16 + (x % 2) * 8 + seq % 8
            pairs.append((fsdp * 16 + seq, target))
    return lax.ppermute(value, ("fsdp", "seq"), pairs)


def gather_groups(piece):
    right, left, far = shift_x(piece, -1), shift_x(piece, 1), shift_x(piece, 2)
    near = jnp.stack([piece, right])
    past = jnp.stack([far, left])
    near_left, near_right = shift_y(near, 1), shift_y(near, -1)
    past_left, past_right = shift_y(past, 1), shift_y(past, -1)
    near_far = shift_y(near_left, 1)
    past_far = shift_y(past_right, -1)
    return (near, near_right, near_far, near_left, past, past_right, past_far, past_left)


def group_kernel(*refs):
    in_refs, out_refs = refs[:4], refs[5:]
    for slot, target in enumerate(out_refs):
        total = sum(ref[slot].astype(F32) for ref in in_refs)
        target[...] = total.astype(target.dtype)


def group_sums(groups, order):
    shape = groups[0].shape[1:]
    outs = (spilled(shape, F32),) + (spilled(shape),) * 3
    return call(
        group_kernel,
        "group_sums",
        outs,
        [full(group) for group in groups] + [anywhere()],
        [full(target) for target in outs],
        grid=(1,),
        flops=10000000000,
    )(*[out(group) for group in groups], out(order))


def scatter_first(groups):
    return [groups[0]] + [shift_y(groups[step], step) for step in range(1, 4)]


def scatter_rest(place, groups, order, packed):
    sums = group_sums(groups, packed)
    ring = [sums[0]] + [shift_x(sums[step], step) for step in range(1, 4)]
    keep, send = z_halves(place, ring, order)
    got = lax.ppermute(send, "seq", [(i, i ^ 4) for i in range(16)])
    parts = list(z_quarters(place, keep, got))
    for step in range(1, 4):
        pairs = [(i, (i & 12) + ((i + step) & 3)) for i in range(16)]
        parts[step] = lax.ppermute(parts[step], "seq", pairs)
    return total_of(parts)


def over_seq(array):
    return lax.all_to_all(array, "seq", split_axis=0, concat_axis=0, tiled=True)


def over_z(array):
    groups = [list(range(8)), list(range(8, 16))]
    return lax.all_to_all(
        array, "seq", split_axis=0, concat_axis=0, axis_index_groups=groups, tiled=True
    )


def join_kernel(place_ref, own_ref, other_ref, order_ref, out_ref):
    first = place_ref[0] == 0
    half = own_ref.shape[1]
    out_ref[:, :half] = jnp.where(first, own_ref[...], other_ref[...])
    out_ref[:, half:] = jnp.where(first, other_ref[...], own_ref[...])


def joined(place, own, other, order, where=out):
    rows, half = own.shape
    return call(
        join_kernel,
        "joined",
        shaped((rows, 2 * half), own.dtype),
        [scalars_spec(), full(own), full(other), anywhere()],
        pl.BlockSpec((rows, 2 * half), lambda i: (0, 0)),
        grid=(1,),
    )(place, where(own), where(other), out(order))


def places():
    cfg = lax.axis_index("cfg")
    fsdp = lax.axis_index("fsdp")
    x = (fsdp >> 2) * 2 + (lax.axis_index("seq") >> 3)
    y = fsdp & 3
    slots = jnp.arange(16)
    there = (x + (slots & 3)) & 3
    block = (there >> 1) * 4 + ((y + (slots >> 2)) & 3)
    table = 2 * block + (there & 1)
    return jnp.concatenate([cfg[None], table, (lax.axis_index("seq") & 7)[None]]).astype(jnp.int32)


def local(query_act, key_act, value_act, out_weight, reward_dir, guide_index, step_index):
    place = places()
    moment = step_index[0].astype(F32)
    gate = jnp.cos(0.5 * jnp.pi * (moment + 0.5) / STEPS)
    strength = 1.0 + GUIDE_STEP * guide_index[0].astype(F32)
    scalars = jnp.stack([gate, strength])
    half = out_weight.shape[1] // 2
    own_half = jnp.where(place[0] == 0, out_weight[:, :half], out_weight[:, half:])
    piece = over_z(jnp.broadcast_to(own_half[None], (8,) + own_half.shape)).reshape(-1, half)
    groups = gather_groups(piece)
    qkv = over_seq(pack_heads(query_act[0, 0], key_act[0, 0], value_act[0, 0]))
    mixed_h, probs = attend_forward(qkv, groups[1], groups[3], groups[5], groups[7], place, scalars)
    mixed = over_seq(mixed_h)
    weight = assemble(place, groups, mixed)
    mixed_other = swap_cfg(mixed)
    guided, grad_out, keep, send = project(
        place, scalars, mixed, mixed_other, reward_dir[0], weight
    )
    grad_mixed = add_after(keep, swap_cfg(send))
    parts = weight_gradient(place, mixed, mixed_other, grad_out, grad_mixed)
    grad_h = over_seq(grad_mixed)
    parts = scatter_first(parts)
    packed = attend_backward(qkv, mixed_h, grad_h, probs, parts[0])
    guided_all = joined(place, guided, swap_cfg(guided), packed)
    last = over_seq(packed)
    grad_half = scatter_rest(place, parts, guided_all, packed)
    grad_query, grad_key, grad_value = unpack_heads(last, 3)
    grad_weight = joined(place, grad_half, swap_cfg(grad_half), grad_query, pin)
    return (
        guided_all[None],
        grad_query[None, None],
        grad_key[None, None],
        grad_value[None, None],
        grad_weight,
    )


def solution(mesh):
    placed = (
        P("cfg", "fsdp", "seq", None),
        P("cfg", "fsdp", "seq", None),
        P("cfg", "fsdp", "seq", None),
        P(("fsdp", "seq"), None),
        P("fsdp", "seq", None),
        P(),
        P(),
    )
    return jax.shard_map(
        local,
        mesh=mesh,
        in_specs=placed,
        out_specs=(
            P("fsdp", "seq", None),
            P("cfg", "fsdp", "seq", None),
            P("cfg", "fsdp", "seq", None),
            P("cfg", "fsdp", "seq", None),
            P(("fsdp", "seq"), None),
        ),
        check_vma=False,
    )
```

```python
import functools

import jax
import jax.numpy as jnp
from jax import lax
from jax.experimental import pallas as pl
from jax.experimental.pallas import tpu as pltpu
from jax.sharding import PartitionSpec as P

HDIM = 128
STEPS = 50
GUIDE_STEP = 0.04
LOG2E = 1.4426950408889634
BF = jnp.bfloat16
F32 = jnp.float32
NT = (((1,), (1,)), ((), ()))
VMEM_LIMIT = 20 * 1024 * 1024


def params():
    return pltpu.CompilerParams(vmem_limit_bytes=VMEM_LIMIT)


def whole(count):
    return [pl.BlockSpec(memory_space=pltpu.VMEM) for _ in range(count)]


def anywhere():
    return pl.BlockSpec(memory_space=pl.ANY)


def full(array):
    rank = len(array.shape)
    return pl.BlockSpec(array.shape, lambda i: (0,) * rank)


def scalars_spec():
    return pl.BlockSpec(memory_space=pltpu.SMEM)


def call(kernel, name, out_shape, in_specs, out_specs=None, flops=1, **kwargs):
    if out_specs is None:
        out_specs = whole(len(out_shape)) if isinstance(out_shape, tuple) else whole(1)[0]
    return pl.pallas_call(
        kernel,
        out_shape=out_shape,
        in_specs=in_specs,
        out_specs=tuple(out_specs) if isinstance(out_shape, tuple) else out_specs,
        compiler_params=params(),
        cost_estimate=pl.CostEstimate(flops=flops, bytes_accessed=1, transcendentals=0),
        name=name,
        **kwargs,
    )


def shaped(shape, dtype=BF):
    return jax.ShapeDtypeStruct(shape, dtype)


def kept(shape, dtype=BF):
    return pltpu.VMEM(shape, dtype)


def pin(array):
    return pltpu.with_memory_space_constraint(array, pltpu.VMEM)


def spilled(shape, dtype=BF):
    return pltpu.HBM(shape, dtype)


def out(array):
    return pltpu.with_memory_space_constraint(array, pltpu.HBM)


def ordered(orders):
    return [anywhere()] * len(orders)


def lanes_of(head):
    return slice(head * HDIM, (head + 1) * HDIM)


def pack_kernel(*refs):
    in_refs, out_ref = refs[:-1], refs[-1]
    rows = in_refs[0].shape[0]
    for head in range(out_ref.shape[0]):
        for place, ref in enumerate(in_refs):
            out_ref[head, place * rows : (place + 1) * rows, :] = ref[:, lanes_of(head)]


def pack_heads(*arrays):
    rows, width = arrays[0].shape
    return call(
        pack_kernel,
        "pack_heads",
        kept((width // HDIM, len(arrays) * rows, HDIM)),
        [full(array) for array in arrays],
        grid=(1,),
    )(*[out(array) for array in arrays])


def unpack_kernel(in_ref, *out_refs):
    rows = out_refs[0].shape[0]
    for head in range(in_ref.shape[0]):
        for place, ref in enumerate(out_refs):
            ref[:, lanes_of(head)] = in_ref[head, place * rows : (place + 1) * rows, :]


def unpack_heads(packed, count):
    target = shaped((packed.shape[1] // count, packed.shape[0] * HDIM))
    return call(
        unpack_kernel,
        "unpack_heads",
        (target,) * count,
        [full(packed)],
        [full(target)] * count,
        grid=(1,),
    )(packed)


CHUNK = 512


def forward_kernel(qkv_ref, *refs):
    out_ref, probs_ref, held, sems = refs[-4:]
    shards, total_rows, _ = qkv_ref.shape
    rows = total_rows // 3
    length = shards * rows
    keys = qkv_ref[:, rows : 2 * rows, :].reshape(length, HDIM)
    value_t = qkv_ref[:, 2 * rows :, :].reshape(length, HDIM).astype(F32).T.astype(BF)
    scale = HDIM ** (-0.5) * LOG2E
    take = CHUNK // rows
    copies = []

    def scores_of(part):
        query = qkv_ref[part * take : (part + 1) * take, :rows, :].reshape(CHUNK, HDIM)
        return lax.dot_general(keys, query, NT, preferred_element_type=F32)

    parts = length // CHUNK
    scores = scores_of(0)
    for part in range(parts):
        later = scores_of(part + 1) if part + 1 < parts else None
        peak = jnp.max(scores, axis=0, keepdims=True) * scale
        weights = jnp.exp2(scores * scale - peak)
        total = jnp.sum(weights, axis=0, keepdims=True)
        probs = (weights * (1.0 / total)).astype(BF)
        lanes = pl.ds(part * CHUNK, CHUNK)
        held[:, lanes] = probs
        copy = pltpu.make_async_copy(held.at[:, lanes], probs_ref.at[:, lanes], sems.at[part])
        copy.start()
        copies.append(copy)
        mixed_t = jnp.dot(value_t, probs, preferred_element_type=F32)
        out_ref[part * take : (part + 1) * take] = mixed_t.T.astype(BF).reshape(take, rows, HDIM)
        scores = later
    for copy in copies:
        copy.wait()


def attend_forward(qkv, *orders):
    shards, total_rows, _ = qkv.shape
    rows = total_rows // 3
    length = shards * rows
    return call(
        forward_kernel,
        "attend_forward",
        (kept((shards, rows, HDIM)), spilled((length, length))),
        whole(1) + ordered(orders),
        whole(1) + [anywhere()],
        scratch_shapes=[
            pltpu.VMEM((length, length), BF),
            pltpu.SemaphoreType.DMA((length // CHUNK,)),
        ],
    )(qkv, *[order if order.ndim == 1 else out(order) for order in orders])


def backward_kernel(qkv_ref, mixed_ref, grad_ref, probs_ref, *refs):
    out_ref, query_t, inner, held, sems = refs[-5:]
    shards, rows, _ = mixed_ref.shape
    length = shards * rows
    factor = HDIM ** (-0.5)
    chunk = CHUNK // 2
    take = chunk // rows

    def fetch(part):
        span = pl.ds(pl.multiple_of(part * CHUNK, CHUNK), CHUNK)
        return pltpu.make_async_copy(probs_ref.at[span], held.at[span], sems.at[part])

    for part in range(length // CHUNK):
        fetch(part).start()
    product = grad_ref[...].astype(F32) * mixed_ref[...].astype(F32)
    inner[...] = jnp.sum(product.reshape(length, HDIM).T, axis=0, keepdims=True)
    query_t[...] = jnp.zeros_like(query_t)

    def one_chunk(part):
        here = pl.ds(part * take, take)
        grad = grad_ref[...].reshape(length, HDIM)
        query = qkv_ref[:, :rows, :].reshape(length, HDIM)
        probs = held[pl.ds(pl.multiple_of(part * chunk, chunk), chunk), :]
        keys = qkv_ref[here, rows : 2 * rows, :].reshape(chunk, HDIM)
        value = qkv_ref[here, 2 * rows :, :].reshape(chunk, HDIM)
        grad_value = jnp.dot(probs, grad, preferred_element_type=F32)
        out_ref[here, 2 * rows :, :] = grad_value.astype(BF).reshape(take, rows, HDIM)
        grad_probs = lax.dot_general(value, grad, NT, preferred_element_type=F32)
        grad_scores = (probs.astype(F32) * (grad_probs - inner[...])).astype(BF)
        grad_key = jnp.dot(grad_scores, query, preferred_element_type=F32) * factor
        out_ref[here, rows : 2 * rows, :] = grad_key.astype(BF).reshape(take, rows, HDIM)
        query_t[...] += jnp.dot(keys.T, grad_scores, preferred_element_type=F32)

    @pl.loop(0, length // CHUNK)
    def _(part):
        fetch(part).wait()
        one_chunk(2 * part)
        one_chunk(2 * part + 1)

    grad_query = (query_t[...] * factor).T.astype(BF)
    out_ref[:, :rows, :] = grad_query.reshape(shards, rows, HDIM)


def attend_backward(qkv, mixed, grad, probs, *orders):
    length = probs.shape[0]
    return call(
        backward_kernel,
        "attend_backward",
        kept(qkv.shape),
        [full(qkv), full(mixed), full(grad), anywhere()] + ordered(orders),
        whole(1)[0],
        grid=(1,),
        flops=16 * length * length * HDIM,
        scratch_shapes=[
            pltpu.VMEM((HDIM, length), F32),
            pltpu.VMEM((1, length), F32),
            pltpu.VMEM((length, length), BF),
            pltpu.SemaphoreType.DMA((length // CHUNK,)),
        ],
    )(out(qkv), out(mixed), grad, out(probs), *[out(order) for order in orders])


def head_of(place_ref, dx, dy):
    return place_ref[1 + 4 * dy + dx]


def head_of(place_ref, dx, dy):
    return place_ref[1 + 4 * dy + dx]


def assemble_kernel(place_ref, *refs):
    groups, out_ref = refs[:-2], refs[-1]
    deep = groups[0].shape[1]
    for dy, (one, two) in enumerate(zip(groups[:4], groups[4:])):
        for dx in range(4):
            start = pl.multiple_of(head_of(place_ref, dx, dy) * deep, deep)
            out_ref[pl.ds(start, deep), :] = (one if dx < 2 else two)[dx % 2]


def assemble(place, groups, order):
    _, deep, wide = groups[0].shape
    return call(
        assemble_kernel,
        "assemble",
        kept((16 * deep, wide)),
        [scalars_spec()] + [full(group) for group in groups] + [anywhere()],
        whole(1)[0],
        grid=(1,),
        flops=10000000000,
    )(place, *[group if i % 4 == 2 else out(group) for i, group in enumerate(groups)], order)


def project_kernel(
    place_ref, scalar_ref, own_ref, other_ref, reward_ref, weight_ref,
    guided_ref, grad_ref, keep_ref, send_ref,
):
    rows = own_ref.shape[1]
    half = guided_ref.shape[1]
    heads = own_ref.shape[0]
    blocks = heads // 2
    deep = 2 * HDIM
    first = place_ref[0] == 0
    gate, strength = scalar_ref[0], scalar_ref[1]
    total = None
    for block in range(blocks):
        head = 2 * block
        columns = jnp.concatenate(
            [
                jnp.concatenate([own_ref[head], own_ref[head + 1]], axis=1),
                jnp.concatenate([other_ref[head], other_ref[head + 1]], axis=1),
            ],
            axis=0,
        )
        part = jnp.dot(
            columns, weight_ref[block * deep : (block + 1) * deep], preferred_element_type=F32
        )
        total = part if total is None else total + part
    branch_out = (gate * total).astype(BF).astype(F32)
    own_out, other_out = branch_out[:rows], branch_out[rows:]
    cond = jnp.where(first, own_out, other_out)
    uncond = jnp.where(first, other_out, own_out)
    guided = uncond + strength * (cond - uncond)
    guided_ref[...] = guided.astype(BF)
    reward = jnp.where(first, reward_ref[:, :half], reward_ref[:, half:]).astype(F32)
    resid = reward - guided
    own_coeff = gate * jnp.where(first, strength, 1.0 - strength)
    other_coeff = gate * jnp.where(first, 1.0 - strength, strength)
    grad = jnp.concatenate([own_coeff * resid, other_coeff * resid], axis=0).astype(BF)
    grad_ref[...] = grad
    for block in range(blocks):
        part = lax.dot_general(
            grad, weight_ref[block * deep : (block + 1) * deep], NT, preferred_element_type=F32
        )
        for odd in range(2):
            lanes = part[:, lanes_of(odd)]
            keep_ref[2 * block + odd] = lanes[:rows]
            send_ref[2 * block + odd] = lanes[rows:].astype(BF)


def project(place, scalars, own, other, reward, weight):
    heads, rows, _ = own.shape
    half = reward.shape[1] // 2
    return call(
        project_kernel,
        "project",
        (
            spilled((rows, half)),
            kept((2 * rows, half)),
            kept((heads, rows, HDIM), F32),
            kept((heads, rows, HDIM)),
        ),
        [scalars_spec(), scalars_spec()] + whole(2) + [full(reward)] + whole(1),
        [pl.BlockSpec((rows, half), lambda i: (0, 0))] + whole(3),
        grid=(1,),
    )(place, scalars, pin(own), pin(other), out(reward), pin(weight))


def weight_kernel(place_ref, own_ref, other_ref, grad_ref, order_ref, *refs):
    grad = grad_ref[...]
    for dy, ref in enumerate(refs):
        for dx in range(4):
            head = head_of(place_ref, dx, dy)
            flipped = jnp.concatenate([own_ref[head].T, other_ref[head].T], axis=1)
            ref[dx] = jnp.dot(flipped, grad, preferred_element_type=F32).astype(BF)


def weight_gradient(place, own, other, grad, order):
    group = spilled((4, HDIM, grad.shape[1]))
    return call(
        weight_kernel,
        "weight_gradient",
        (group,) * 4,
        [scalars_spec()] + whole(3) + [anywhere()],
        [full(group)] * 4,
        grid=(1,),
    )(place, pin(own), pin(other), pin(grad), order)


def add_kernel(keep_ref, got_ref, out_ref):
    out_ref[...] = (keep_ref[...] + got_ref[...].astype(F32)).astype(BF)


def add_after(keep, got):
    return call(add_kernel, "add_after", kept(got.shape), whole(2))(pin(keep), pin(got))


def quads_kernel(place_ref, *refs):
    arrays, out_refs, held = refs[:4], refs[5:-1], refs[-1]
    deep = out_refs[0].shape[1]
    held[...] = sum(ref[...].astype(F32) for ref in arrays)
    for step, ref in enumerate(out_refs):
        low = (place_ref[17] + step) & 3
        for high in range(2):
            start = pl.multiple_of((4 * high + low) * deep, deep)
            ref[high] = held[pl.ds(start, deep), :].astype(ref.dtype)


def z_quads(place, arrays, order):
    rows, wide = arrays[0].shape
    target = (2, rows // 8, wide)
    return call(
        quads_kernel,
        "z_quads",
        (kept(target, F32),) + (kept(target),) * 3,
        [scalars_spec()] + [full(array) for array in arrays] + [anywhere()],
        whole(4),
        grid=(1,),
        flops=10000000000,
        scratch_shapes=[pltpu.VMEM((rows, wide), F32)],
    )(place, *[out(array) for array in arrays], out(order))


def pair_kernel(place_ref, *refs):
    in_refs, keep_ref, send_ref = refs[:4], refs[4], refs[5]
    total = sum(ref[...].astype(F32) for ref in in_refs)
    first = (place_ref[17] >> 2) == 0
    keep_ref[...] = jnp.where(first, total[0], total[1])
    send_ref[...] = jnp.where(first, total[1], total[0]).astype(BF)


def z_pair(place, parts):
    shape = parts[0].shape[1:]
    return call(
        pair_kernel,
        "z_pair",
        (kept(shape, F32), kept(shape)),
        [scalars_spec()] + whole(4),
    )(place, *[pin(part) for part in parts])


def total_kernel(*refs):
    in_refs, out_ref = refs[:-1], refs[-1]
    out_ref[...] = sum(ref[...].astype(F32) for ref in in_refs)


def total_of(arrays):
    return call(
        total_kernel,
        "total_of",
        kept(arrays[0].shape, F32),
        whole(len(arrays)),
        whole(1)[0],
    )(*[pin(array) for array in arrays])


def spread_kernel(weight_ref, out_ref):
    half = out_ref.shape[2]
    first = lax.axis_index("cfg") == 0
    own = jnp.where(first, weight_ref[:, :half], weight_ref[:, half:])
    for target in range(out_ref.shape[0]):
        out_ref[target] = own


def spread(weight):
    rows, width = weight.shape
    return call(
        spread_kernel,
        "spread",
        spilled((8, rows, width // 2)),
        [full(weight)],
        pl.BlockSpec((8, rows, width // 2), lambda i: (0, 0, 0)),
        grid=(1,),
    )(out(weight))


def swap_cfg(value):
    return lax.ppermute(value, "cfg", [(0, 1), (1, 0)])


def shift_y(value, step):
    pairs = [(i, (i // 4) * 4 + (i % 4 + step) % 4) for i in range(8)]
    return lax.ppermute(value, "fsdp", pairs)


def shift_x(value, step):
    pairs = []
    for fsdp in range(8):
        for seq in range(16):
            x = ((fsdp // 4) * 2 + seq // 8 + step) % 4
            target = ((x // 2) * 4 + fsdp % 4) * 16 + (x % 2) * 8 + seq % 8
            pairs.append((fsdp * 16 + seq, target))
    return lax.ppermute(value, ("fsdp", "seq"), pairs)


def gather_groups(piece):
    right, left, far = shift_x(piece, -1), shift_x(piece, 1), shift_x(piece, 2)
    near = jnp.stack([piece, right])
    past = jnp.stack([far, left])
    near_left, near_right = shift_y(near, 1), shift_y(near, -1)
    past_left, past_right = shift_y(past, 1), shift_y(past, -1)
    near_far = shift_y(near_left, 1)
    past_far = shift_y(past_right, -1)
    return (near, near_right, near_far, near_left, past, past_right, past_far, past_left)


def group_kernel(*refs):
    in_refs, out_refs = refs[:4], refs[5:]
    for slot, target in enumerate(out_refs):
        total = sum(ref[slot].astype(F32) for ref in in_refs)
        target[...] = total.astype(target.dtype)


def group_sums(groups, order):
    shape = groups[0].shape[1:]
    outs = (spilled(shape, F32),) + (spilled(shape),) * 3
    return call(
        group_kernel,
        "group_sums",
        outs,
        [full(group) for group in groups] + [anywhere()],
        [full(target) for target in outs],
        grid=(1,),
        flops=10000000000,
    )(*[out(group) for group in groups], out(order))


def scatter_first(groups):
    return [groups[0]] + [shift_y(groups[step], step) for step in range(1, 4)]


def scatter_rest(place, groups, order, packed):
    sums = group_sums(groups, packed)
    ring = [sums[0]] + [shift_x(sums[step], step) for step in range(1, 4)]
    parts = list(z_quads(place, ring, order))
    for step in range(1, 4):
        pairs = [(i, (i & 12) + ((i + step) & 3)) for i in range(16)]
        parts[step] = lax.ppermute(parts[step], "seq", pairs)
    keep, send = z_pair(place, parts)
    return total_of([keep, lax.ppermute(send, "seq", [(i, i ^ 4) for i in range(16)])])


def over_seq(array):
    return lax.all_to_all(array, "seq", split_axis=0, concat_axis=0, tiled=True)


def over_z(array):
    groups = [list(range(8)), list(range(8, 16))]
    return lax.all_to_all(
        array, "seq", split_axis=0, concat_axis=0, axis_index_groups=groups, tiled=True
    )


def join_kernel(place_ref, own_ref, other_ref, order_ref, out_ref):
    first = place_ref[0] == 0
    half = own_ref.shape[1]
    out_ref[:, :half] = jnp.where(first, own_ref[...], other_ref[...])
    out_ref[:, half:] = jnp.where(first, other_ref[...], own_ref[...])


def joined(place, own, other, order, where=out):
    rows, half = own.shape
    return call(
        join_kernel,
        "joined",
        shaped((rows, 2 * half), own.dtype),
        [scalars_spec(), full(own), full(other), anywhere()],
        pl.BlockSpec((rows, 2 * half), lambda i: (0, 0)),
        grid=(1,),
    )(place, where(own), where(other), out(order))


def places():
    cfg = lax.axis_index("cfg")
    fsdp = lax.axis_index("fsdp")
    x = (fsdp >> 2) * 2 + (lax.axis_index("seq") >> 3)
    y = fsdp & 3
    slots = jnp.arange(16)
    there = (x + (slots & 3)) & 3
    block = (there >> 1) * 4 + ((y + (slots >> 2)) & 3)
    table = 2 * block + (there & 1)
    return jnp.concatenate([cfg[None], table, (lax.axis_index("seq") & 7)[None]]).astype(jnp.int32)


def local(query_act, key_act, value_act, out_weight, reward_dir, guide_index, step_index):
    place = places()
    moment = step_index[0].astype(F32)
    gate = jnp.cos(0.5 * jnp.pi * (moment + 0.5) / STEPS)
    strength = 1.0 + GUIDE_STEP * guide_index[0].astype(F32)
    scalars = jnp.stack([gate, strength])
    half = out_weight.shape[1] // 2
    piece = over_z(spread(out_weight)).reshape(-1, half)
    groups = gather_groups(piece)
    qkv = over_seq(pack_heads(query_act[0, 0], key_act[0, 0], value_act[0, 0]))
    mixed_h, probs = attend_forward(qkv, groups[1], groups[3], groups[5], groups[7], place, scalars)
    mixed = over_seq(mixed_h)
    weight = assemble(place, groups, mixed)
    mixed_other = swap_cfg(mixed)
    guided, grad_out, keep, send = project(
        place, scalars, mixed, mixed_other, reward_dir[0], weight
    )
    grad_mixed = add_after(keep, swap_cfg(send))
    parts = weight_gradient(place, mixed, mixed_other, grad_out, grad_mixed)
    grad_h = over_seq(grad_mixed)
    parts = scatter_first(parts)
    packed = attend_backward(qkv, mixed_h, grad_h, probs, parts[0])
    guided_all = joined(place, guided, swap_cfg(guided), packed)
    last = over_seq(packed)
    grad_half = scatter_rest(place, parts, guided_all, packed)
    grad_query, grad_key, grad_value = unpack_heads(last, 3)
    grad_weight = joined(place, grad_half, swap_cfg(grad_half), grad_query, pin)
    return (
        guided_all[None],
        grad_query[None, None],
        grad_key[None, None],
        grad_value[None, None],
        grad_weight,
    )


def solution(mesh):
    placed = (
        P("cfg", "fsdp", "seq", None),
        P("cfg", "fsdp", "seq", None),
        P("cfg", "fsdp", "seq", None),
        P(("fsdp", "seq"), None),
        P("fsdp", "seq", None),
        P(),
        P(),
    )
    return jax.shard_map(
        local,
        mesh=mesh,
        in_specs=placed,
        out_specs=(
            P("fsdp", "seq", None),
            P("cfg", "fsdp", "seq", None),
            P("cfg", "fsdp", "seq", None),
            P("cfg", "fsdp", "seq", None),
            P(("fsdp", "seq"), None),
        ),
        check_vma=False,
    )
```

```python
import functools

import jax
import jax.numpy as jnp
from jax import lax
from jax.experimental import pallas as pl
from jax.experimental.pallas import tpu as pltpu
from jax.sharding import PartitionSpec as P

HDIM = 128
STEPS = 50
GUIDE_STEP = 0.04
LOG2E = 1.4426950408889634
BF = jnp.bfloat16
F32 = jnp.float32
NT = (((1,), (1,)), ((), ()))
VMEM_LIMIT = 20 * 1024 * 1024


def params():
    return pltpu.CompilerParams(vmem_limit_bytes=VMEM_LIMIT)


def whole(count):
    return [pl.BlockSpec(memory_space=pltpu.VMEM) for _ in range(count)]


def anywhere():
    return pl.BlockSpec(memory_space=pl.ANY)


def full(array):
    rank = len(array.shape)
    return pl.BlockSpec(array.shape, lambda i: (0,) * rank)


def scalars_spec():
    return pl.BlockSpec(memory_space=pltpu.SMEM)


def call(kernel, name, out_shape, in_specs, out_specs=None, flops=1, **kwargs):
    if out_specs is None:
        out_specs = whole(len(out_shape)) if isinstance(out_shape, tuple) else whole(1)[0]
    return pl.pallas_call(
        kernel,
        out_shape=out_shape,
        in_specs=in_specs,
        out_specs=tuple(out_specs) if isinstance(out_shape, tuple) else out_specs,
        compiler_params=params(),
        cost_estimate=pl.CostEstimate(flops=flops, bytes_accessed=1, transcendentals=0),
        name=name,
        **kwargs,
    )


def shaped(shape, dtype=BF):
    return jax.ShapeDtypeStruct(shape, dtype)


def kept(shape, dtype=BF):
    return pltpu.VMEM(shape, dtype)


def pin(array):
    return pltpu.with_memory_space_constraint(array, pltpu.VMEM)


def spilled(shape, dtype=BF):
    return pltpu.HBM(shape, dtype)


def out(array):
    return pltpu.with_memory_space_constraint(array, pltpu.HBM)


def ordered(orders):
    return [anywhere()] * len(orders)


def lanes_of(head):
    return slice(head * HDIM, (head + 1) * HDIM)


def pack_kernel(*refs):
    in_refs, out_ref = refs[:-1], refs[-1]
    rows = in_refs[0].shape[0]
    for head in range(out_ref.shape[0]):
        for place, ref in enumerate(in_refs):
            out_ref[head, place * rows : (place + 1) * rows, :] = ref[:, lanes_of(head)]


def pack_heads(*arrays):
    rows, width = arrays[0].shape
    return call(
        pack_kernel,
        "pack_heads",
        kept((width // HDIM, len(arrays) * rows, HDIM)),
        [full(array) for array in arrays],
        grid=(1,),
    )(*[out(array) for array in arrays])


def unpack_kernel(in_ref, *out_refs):
    rows = out_refs[0].shape[0]
    for head in range(in_ref.shape[0]):
        for place, ref in enumerate(out_refs):
            ref[:, lanes_of(head)] = in_ref[head, place * rows : (place + 1) * rows, :]


def unpack_heads(packed, count):
    target = shaped((packed.shape[1] // count, packed.shape[0] * HDIM))
    return call(
        unpack_kernel,
        "unpack_heads",
        (target,) * count,
        [full(packed)],
        [full(target)] * count,
        grid=(1,),
    )(packed)


CHUNK = 512


def forward_kernel(qkv_ref, *refs):
    out_ref, probs_ref, held, sems = refs[-4:]
    shards, total_rows, _ = qkv_ref.shape
    rows = total_rows // 3
    length = shards * rows
    keys = qkv_ref[:, rows : 2 * rows, :].reshape(length, HDIM)
    value_t = qkv_ref[:, 2 * rows :, :].reshape(length, HDIM).T
    scale = HDIM ** (-0.5) * LOG2E
    take = CHUNK // rows
    copies = []

    def scores_of(part):
        query = qkv_ref[part * take : (part + 1) * take, :rows, :].reshape(CHUNK, HDIM)
        return lax.dot_general(keys, query, NT, preferred_element_type=F32)

    parts = length // CHUNK
    scores = scores_of(0)
    for part in range(parts):
        later = scores_of(part + 1) if part + 1 < parts else None
        peak = jnp.max(scores, axis=0, keepdims=True) * scale
        weights = jnp.exp2(scores * scale - peak)
        total = jnp.sum(weights, axis=0, keepdims=True)
        probs = (weights * (1.0 / total)).astype(BF)
        lanes = pl.ds(part * CHUNK, CHUNK)
        held[:, lanes] = probs
        copy = pltpu.make_async_copy(held.at[:, lanes], probs_ref.at[:, lanes], sems.at[part])
        copy.start()
        copies.append(copy)
        mixed_t = jnp.dot(value_t, probs, preferred_element_type=F32)
        out_ref[part * take : (part + 1) * take] = mixed_t.astype(BF).T.reshape(take, rows, HDIM)
        scores = later
    for copy in copies:
        copy.wait()


def attend_forward(qkv, *orders):
    shards, total_rows, _ = qkv.shape
    rows = total_rows // 3
    length = shards * rows
    return call(
        forward_kernel,
        "attend_forward",
        (kept((shards, rows, HDIM)), spilled((length, length))),
        whole(1) + ordered(orders),
        whole(1) + [anywhere()],
        scratch_shapes=[
            pltpu.VMEM((length, length), BF),
            pltpu.SemaphoreType.DMA((length // CHUNK,)),
        ],
    )(qkv, *[order if order.ndim == 1 else out(order) for order in orders])


def backward_kernel(qkv_ref, mixed_ref, grad_ref, probs_ref, *refs):
    out_ref, query_t, inner, held, sems = refs[-5:]
    shards, rows, _ = mixed_ref.shape
    length = shards * rows
    factor = HDIM ** (-0.5)
    chunk = CHUNK // 2
    take = chunk // rows

    def fetch(part):
        span = pl.ds(pl.multiple_of(part * CHUNK, CHUNK), CHUNK)
        return pltpu.make_async_copy(probs_ref.at[span], held.at[span], sems.at[part])

    for part in range(length // CHUNK):
        fetch(part).start()
    product = grad_ref[...].astype(F32) * mixed_ref[...].astype(F32)
    inner[...] = jnp.sum(product.reshape(length, HDIM).T, axis=0, keepdims=True)
    query_t[...] = jnp.zeros_like(query_t)

    def one_chunk(part):
        here = pl.ds(part * take, take)
        grad = grad_ref[...].reshape(length, HDIM)
        query = qkv_ref[:, :rows, :].reshape(length, HDIM)
        probs = held[pl.ds(pl.multiple_of(part * chunk, chunk), chunk), :]
        keys = qkv_ref[here, rows : 2 * rows, :].reshape(chunk, HDIM)
        value = qkv_ref[here, 2 * rows :, :].reshape(chunk, HDIM)
        grad_value = jnp.dot(probs, grad, preferred_element_type=F32)
        out_ref[here, 2 * rows :, :] = grad_value.astype(BF).reshape(take, rows, HDIM)
        grad_probs = lax.dot_general(value, grad, NT, preferred_element_type=F32)
        grad_scores = (probs.astype(F32) * (grad_probs - inner[...])).astype(BF)
        grad_key = jnp.dot(grad_scores, query, preferred_element_type=F32) * factor
        out_ref[here, rows : 2 * rows, :] = grad_key.astype(BF).reshape(take, rows, HDIM)
        query_t[...] += jnp.dot(keys.T, grad_scores, preferred_element_type=F32)

    @pl.loop(0, length // CHUNK)
    def _(part):
        fetch(part).wait()
        one_chunk(2 * part)
        one_chunk(2 * part + 1)

    grad_query = (query_t[...] * factor).astype(BF).T
    out_ref[:, :rows, :] = grad_query.reshape(shards, rows, HDIM)


def attend_backward(qkv, mixed, grad, probs, *orders):
    length = probs.shape[0]
    return call(
        backward_kernel,
        "attend_backward",
        kept(qkv.shape),
        [full(qkv), full(mixed), full(grad), anywhere()] + ordered(orders),
        whole(1)[0],
        grid=(1,),
        flops=16 * length * length * HDIM,
        scratch_shapes=[
            pltpu.VMEM((HDIM, length), F32),
            pltpu.VMEM((1, length), F32),
            pltpu.VMEM((length, length), BF),
            pltpu.SemaphoreType.DMA((length // CHUNK,)),
        ],
    )(out(qkv), out(mixed), grad, out(probs), *[out(order) for order in orders])


def head_of(place_ref, dx, dy):
    return place_ref[1 + 4 * dy + dx]


def head_of(place_ref, dx, dy):
    return place_ref[1 + 4 * dy + dx]


def assemble_kernel(place_ref, *refs):
    groups, out_ref = refs[:-2], refs[-1]
    deep = groups[0].shape[1]
    for dy, (one, two) in enumerate(zip(groups[:4], groups[4:])):
        for dx in range(4):
            start = pl.multiple_of(head_of(place_ref, dx, dy) * deep, deep)
            out_ref[pl.ds(start, deep), :] = (one if dx < 2 else two)[dx % 2]


def assemble(place, groups, order):
    _, deep, wide = groups[0].shape
    return call(
        assemble_kernel,
        "assemble",
        kept((16 * deep, wide)),
        [scalars_spec()] + [full(group) for group in groups] + [anywhere()],
        whole(1)[0],
        grid=(1,),
        flops=10000000000,
    )(place, *[group if i % 4 == 2 else out(group) for i, group in enumerate(groups)], order)


def project_kernel(
    place_ref, scalar_ref, own_ref, other_ref, reward_ref, weight_ref,
    guided_ref, grad_ref, keep_ref, send_ref,
):
    rows = own_ref.shape[1]
    half = guided_ref.shape[1]
    heads = own_ref.shape[0]
    blocks = heads // 2
    deep = 2 * HDIM
    first = place_ref[0] == 0
    gate, strength = scalar_ref[0], scalar_ref[1]
    total = None
    for block in range(blocks):
        head = 2 * block
        columns = jnp.concatenate(
            [
                jnp.concatenate([own_ref[head], own_ref[head + 1]], axis=1),
                jnp.concatenate([other_ref[head], other_ref[head + 1]], axis=1),
            ],
            axis=0,
        )
        part = jnp.dot(
            columns, weight_ref[block * deep : (block + 1) * deep], preferred_element_type=F32
        )
        total = part if total is None else total + part
    branch_out = (gate * total).astype(BF).astype(F32)
    own_out, other_out = branch_out[:rows], branch_out[rows:]
    cond = jnp.where(first, own_out, other_out)
    uncond = jnp.where(first, other_out, own_out)
    guided = uncond + strength * (cond - uncond)
    guided_ref[...] = guided.astype(BF)
    reward = jnp.where(first, reward_ref[:, :half], reward_ref[:, half:]).astype(F32)
    resid = reward - guided
    own_coeff = gate * jnp.where(first, strength, 1.0 - strength)
    other_coeff = gate * jnp.where(first, 1.0 - strength, strength)
    grad = jnp.concatenate([own_coeff * resid, other_coeff * resid], axis=0).astype(BF)
    grad_ref[...] = grad
    for block in range(blocks):
        part = lax.dot_general(
            grad, weight_ref[block * deep : (block + 1) * deep], NT, preferred_element_type=F32
        )
        for odd in range(2):
            lanes = part[:, lanes_of(odd)]
            keep_ref[2 * block + odd] = lanes[:rows]
            send_ref[2 * block + odd] = lanes[rows:].astype(BF)


def project(place, scalars, own, other, reward, weight):
    heads, rows, _ = own.shape
    half = reward.shape[1] // 2
    return call(
        project_kernel,
        "project",
        (
            spilled((rows, half)),
            kept((2 * rows, half)),
            kept((heads, rows, HDIM), F32),
            kept((heads, rows, HDIM)),
        ),
        [scalars_spec(), scalars_spec()] + whole(2) + [full(reward)] + whole(1),
        [pl.BlockSpec((rows, half), lambda i: (0, 0))] + whole(3),
        grid=(1,),
    )(place, scalars, pin(own), pin(other), out(reward), pin(weight))


def weight_kernel(place_ref, own_ref, other_ref, grad_ref, order_ref, *refs):
    grad = grad_ref[...]
    for dy, ref in enumerate(refs):
        for dx in range(4):
            head = head_of(place_ref, dx, dy)
            flipped = jnp.concatenate([own_ref[head].T, other_ref[head].T], axis=1)
            ref[dx] = jnp.dot(flipped, grad, preferred_element_type=F32).astype(BF)


def weight_gradient(place, own, other, grad, order):
    group = spilled((4, HDIM, grad.shape[1]))
    return call(
        weight_kernel,
        "weight_gradient",
        (group,) * 4,
        [scalars_spec()] + whole(3) + [anywhere()],
        [full(group)] * 4,
        grid=(1,),
    )(place, pin(own), pin(other), pin(grad), order)


def add_kernel(keep_ref, got_ref, out_ref):
    out_ref[...] = (keep_ref[...] + got_ref[...].astype(F32)).astype(BF)


def add_after(keep, got):
    return call(add_kernel, "add_after", kept(got.shape), whole(2))(pin(keep), pin(got))


def quads_kernel(place_ref, *refs):
    arrays, out_refs, held = refs[:4], refs[5:-1], refs[-1]
    deep = out_refs[0].shape[1]
    held[...] = sum(ref[...].astype(F32) for ref in arrays)
    for step, ref in enumerate(out_refs):
        low = (place_ref[17] + step) & 3
        for high in range(2):
            start = pl.multiple_of((4 * high + low) * deep, deep)
            ref[high] = held[pl.ds(start, deep), :].astype(ref.dtype)


def z_quads(place, arrays, order):
    rows, wide = arrays[0].shape
    target = (2, rows // 8, wide)
    return call(
        quads_kernel,
        "z_quads",
        (kept(target, F32),) + (kept(target),) * 3,
        [scalars_spec()] + [full(array) for array in arrays] + [anywhere()],
        whole(4),
        grid=(1,),
        flops=10000000000,
        scratch_shapes=[pltpu.VMEM((rows, wide), F32)],
    )(place, *[out(array) for array in arrays], out(order))


def pair_kernel(place_ref, *refs):
    in_refs, keep_ref, send_ref = refs[:4], refs[4], refs[5]
    total = sum(ref[...].astype(F32) for ref in in_refs)
    first = (place_ref[17] >> 2) == 0
    keep_ref[...] = jnp.where(first, total[0], total[1])
    send_ref[...] = jnp.where(first, total[1], total[0]).astype(BF)


def z_pair(place, parts):
    shape = parts[0].shape[1:]
    return call(
        pair_kernel,
        "z_pair",
        (kept(shape, F32), kept(shape)),
        [scalars_spec()] + whole(4),
    )(place, *[pin(part) for part in parts])


def total_kernel(*refs):
    in_refs, out_ref = refs[:-1], refs[-1]
    out_ref[...] = sum(ref[...].astype(F32) for ref in in_refs)


def total_of(arrays):
    return call(
        total_kernel,
        "total_of",
        kept(arrays[0].shape, F32),
        whole(len(arrays)),
        whole(1)[0],
    )(*[pin(array) for array in arrays])


def spread_kernel(weight_ref, out_ref):
    half = out_ref.shape[2]
    first = lax.axis_index("cfg") == 0
    own = jnp.where(first, weight_ref[:, :half], weight_ref[:, half:])
    for target in range(out_ref.shape[0]):
        out_ref[target] = own


def spread(weight):
    rows, width = weight.shape
    return call(
        spread_kernel,
        "spread",
        spilled((8, rows, width // 2)),
        [full(weight)],
        pl.BlockSpec((8, rows, width // 2), lambda i: (0, 0, 0)),
        grid=(1,),
    )(out(weight))


def swap_cfg(value):
    return lax.ppermute(value, "cfg", [(0, 1), (1, 0)])


def shift_y(value, step):
    pairs = [(i, (i // 4) * 4 + (i % 4 + step) % 4) for i in range(8)]
    return lax.ppermute(value, "fsdp", pairs)


def shift_x(value, step):
    pairs = []
    for fsdp in range(8):
        for seq in range(16):
            x = ((fsdp // 4) * 2 + seq // 8 + step) % 4
            target = ((x // 2) * 4 + fsdp % 4) * 16 + (x % 2) * 8 + seq % 8
            pairs.append((fsdp * 16 + seq, target))
    return lax.ppermute(value, ("fsdp", "seq"), pairs)


def gather_groups(piece):
    right, left, far = shift_x(piece, -1), shift_x(piece, 1), shift_x(piece, 2)
    near = jnp.stack([piece, right])
    past = jnp.stack([far, left])
    near_left, near_right = shift_y(near, 1), shift_y(near, -1)
    past_left, past_right = shift_y(past, 1), shift_y(past, -1)
    near_far = shift_y(near_left, 1)
    past_far = shift_y(past_right, -1)
    return (near, near_right, near_far, near_left, past, past_right, past_far, past_left)


def group_kernel(*refs):
    in_refs, out_refs = refs[:4], refs[5:]
    for slot, target in enumerate(out_refs):
        total = sum(ref[slot].astype(F32) for ref in in_refs)
        target[...] = total.astype(target.dtype)


def group_sums(groups, order):
    shape = groups[0].shape[1:]
    outs = (spilled(shape, F32),) + (spilled(shape),) * 3
    return call(
        group_kernel,
        "group_sums",
        outs,
        [full(group) for group in groups] + [anywhere()],
        [full(target) for target in outs],
        grid=(1,),
        flops=10000000000,
    )(*[out(group) for group in groups], out(order))


def scatter_first(groups):
    return [groups[0]] + [shift_y(groups[step], step) for step in range(1, 4)]


def scatter_rest(place, groups, order, packed):
    sums = group_sums(groups, packed)
    ring = [sums[0]] + [shift_x(sums[step], step) for step in range(1, 4)]
    parts = list(z_quads(place, ring, order))
    for step in range(1, 4):
        pairs = [(i, (i & 12) + ((i + step) & 3)) for i in range(16)]
        parts[step] = lax.ppermute(parts[step], "seq", pairs)
    keep, send = z_pair(place, parts)
    return total_of([keep, lax.ppermute(send, "seq", [(i, i ^ 4) for i in range(16)])])


def over_seq(array):
    return lax.all_to_all(array, "seq", split_axis=0, concat_axis=0, tiled=True)


def over_z(array):
    groups = [list(range(8)), list(range(8, 16))]
    return lax.all_to_all(
        array, "seq", split_axis=0, concat_axis=0, axis_index_groups=groups, tiled=True
    )


def join_kernel(place_ref, own_ref, other_ref, order_ref, out_ref):
    first = place_ref[0] == 0
    half = own_ref.shape[1]
    out_ref[:, :half] = jnp.where(first, own_ref[...], other_ref[...])
    out_ref[:, half:] = jnp.where(first, other_ref[...], own_ref[...])


def joined(place, own, other, order, where=out):
    rows, half = own.shape
    return call(
        join_kernel,
        "joined",
        shaped((rows, 2 * half), own.dtype),
        [scalars_spec(), full(own), full(other), anywhere()],
        pl.BlockSpec((rows, 2 * half), lambda i: (0, 0)),
        grid=(1,),
    )(place, where(own), where(other), out(order))


def places():
    cfg = lax.axis_index("cfg")
    fsdp = lax.axis_index("fsdp")
    x = (fsdp >> 2) * 2 + (lax.axis_index("seq") >> 3)
    y = fsdp & 3
    slots = jnp.arange(16)
    there = (x + (slots & 3)) & 3
    block = (there >> 1) * 4 + ((y + (slots >> 2)) & 3)
    table = 2 * block + (there & 1)
    return jnp.concatenate([cfg[None], table, (lax.axis_index("seq") & 7)[None]]).astype(jnp.int32)


def local(query_act, key_act, value_act, out_weight, reward_dir, guide_index, step_index):
    place = places()
    moment = step_index[0].astype(F32)
    gate = jnp.cos(0.5 * jnp.pi * (moment + 0.5) / STEPS)
    strength = 1.0 + GUIDE_STEP * guide_index[0].astype(F32)
    scalars = jnp.stack([gate, strength])
    half = out_weight.shape[1] // 2
    piece = over_z(spread(out_weight)).reshape(-1, half)
    groups = gather_groups(piece)
    qkv = over_seq(pack_heads(query_act[0, 0], key_act[0, 0], value_act[0, 0]))
    mixed_h, probs = attend_forward(qkv, groups[1], groups[3], groups[5], groups[7], place, scalars)
    mixed = over_seq(mixed_h)
    weight = assemble(place, groups, mixed)
    mixed_other = swap_cfg(mixed)
    guided, grad_out, keep, send = project(
        place, scalars, mixed, mixed_other, reward_dir[0], weight
    )
    grad_mixed = add_after(keep, swap_cfg(send))
    parts = weight_gradient(place, mixed, mixed_other, grad_out, grad_mixed)
    grad_h = over_seq(grad_mixed)
    parts = scatter_first(parts)
    packed = attend_backward(qkv, mixed_h, grad_h, probs, parts[0])
    guided_all = joined(place, guided, swap_cfg(guided), packed)
    last = over_seq(packed)
    grad_half = scatter_rest(place, parts, guided_all, packed)
    grad_query, grad_key, grad_value = unpack_heads(last, 3)
    grad_weight = joined(place, grad_half, swap_cfg(grad_half), grad_query, pin)
    return (
        guided_all[None],
        grad_query[None, None],
        grad_key[None, None],
        grad_value[None, None],
        grad_weight,
    )


def solution(mesh):
    placed = (
        P("cfg", "fsdp", "seq", None),
        P("cfg", "fsdp", "seq", None),
        P("cfg", "fsdp", "seq", None),
        P(("fsdp", "seq"), None),
        P("fsdp", "seq", None),
        P(),
        P(),
    )
    return jax.shard_map(
        local,
        mesh=mesh,
        in_specs=placed,
        out_specs=(
            P("fsdp", "seq", None),
            P("cfg", "fsdp", "seq", None),
            P("cfg", "fsdp", "seq", None),
            P("cfg", "fsdp", "seq", None),
            P(("fsdp", "seq"), None),
        ),
        check_vma=False,
    )
```
